256 devices in a mesh: seq: 32 (over x, y, core), mp: 8 (over z).
Axes of the slice: x: 4, y: 4, z: 8, core: 2. Of those that a mesh axis runs over, the one named last changes fastest.
Arguments:
- tokens: bfloat16 [20480, 1024], P('seq'), may hold values from -6 to 6
- block_modality: int32 [160], P('seq'), may hold values from 0 to 2
- live_blocks: int32 [32], P('seq'), may hold values from 1 to 5, 100 in all
- mode_table: float32 [3, 1024], replicated, may hold values from -5 to 5
- latents: bfloat16 [2048, 4096], P('seq'), may hold values from -6 to 6
- w_query: bfloat16 [4096, 4096], P(None, 'mp'), may hold values from -1 to 1
- w_key: bfloat16 [1024, 4096], P(None, 'mp'), may hold values from -1 to 1
- w_value: bfloat16 [1024, 4096], P(None, 'mp'), may hold values from -0.1875 to 0.1875
- w_out: bfloat16 [4096, 4096], P('mp'), may hold values from -0.375 to 0.375
- cotangent: bfloat16 [2048, 4096], P('seq'), may hold values from -6 to 6
Outputs:
- mixed: bfloat16 [2048, 4096], P('seq')
- grad_key: float32 [1024, 4096], P('seq', 'mp')
- grad_value: float32 [1024, 4096], P('seq', 'mp')
The draws below stay inside these ranges and needn't reach their ends.
Inputs may be any that keep to these rules, and one draw needn't show every extreme that they name: `live_blocks`: some index of seq has exactly 5 live blocks.
All inputs are finite; a program needn't handle non-finite values.
Results may differ from the reference program's by a relative error of at most 0.04.
The reference program's roundings to bfloat16 on the way (of `normed`, `attn` and `back`) count: a program that leaves them out, or rounds other values in their place, can miss the bound.
Values may be sent and summed in bfloat16 or wider, within the bound.
No kernel may reach another device: no remote copies, remote signals or barrier semaphores. Data moves between devices by JAX's collectives and lax.ppermute only.
A program may use at most 128 MiB of HBM per device.

```python
import math
import jax
import jax.numpy as jnp
import numpy as np
from jax import lax

DIN = 1024
DL = 4096
LAT = 2048
HEADS = 8
MODES = 3
TOK_DEV = 640
HD = 512
BLK_DEV = 5
TOKENS = 20480
NBLK = 160
LIVE = 100
N_SEQ = 32


def draw_w_query(key, part):
    key = jax.random.fold_in(key, 3)
    result = jax.random.normal(key, (DL, DL), jnp.float32) * DL ** (-0.5)
    return jnp.clip(result, -1.0, 1.0).astype(jnp.bfloat16)


def draw_w_key(key, part):
    key = jax.random.fold_in(key, 5)
    result = jax.random.normal(key, (DIN, DL), jnp.float32) * DIN ** (-0.5)
    return jnp.clip(result, -1.0, 1.0).astype(jnp.bfloat16)


def set_ends(values, own_key, low, high):
    index_at = [jax.random.randint(jax.random.fold_in(own_key, axis), (), 0, length) for axis, length in enumerate(values.shape)]
    widest = values.shape.index(max(values.shape))
    neighbour = index_at[:widest] + [(index_at[widest] + 1) % values.shape[widest]] + index_at[widest + 1:]
    return values.at[tuple(index_at)].set(low).at[tuple(neighbour)].set(high)


def strengthened(values, stream_key, source, target, shards_of, factor):
    owner, partner = [(jnp.arange(values.shape[dim]) // (values.shape[dim] // shards_of)).reshape([-1 if axis == dim else 1 for axis in range(values.ndim)]) for dim in (source, target)]
    chosen = jax.random.permutation(stream_key, shards_of)[partner]
    strong = (owner == chosen) | (owner == (partner + shards_of // 2) % shards_of)
    return jnp.where(strong, factor * values, values)


def levels(own_key, shape, shards, smallest, top_value):
    def one(dim, shards_of):
        draws = jax.random.uniform(jax.random.fold_in(jax.random.fold_in(own_key, 6), dim), (shards_of,), jnp.float32, smallest / len(shards), top_value / len(shards))
        return jnp.repeat(jnp.exp(draws), shape[dim] // shards_of).reshape((-1,) + (1,) * (len(shape) - dim - 1))

    loudness = one(*shards[0])
    for cut in shards[1:]:
        loudness = loudness * one(*cut)
    return loudness


def length_profile(number_of, total, reach, slope):
    loads = [(1 << 20) // math.isqrt(grade ** slope) + 1 for grade in range(2, number_of + 1)]
    surplus, counts = total - reach - (number_of - 1), [1] * (number_of - 1)
    while surplus > 0:
        free = [i for i in range(number_of - 1) if counts[i] < reach]
        whole, budget = sum([loads[i] for i in free]), surplus
        for i in free:
            more = min(reach - counts[i], max(1, budget * loads[i] // whole), surplus)
            counts[i] = counts[i] + more
            surplus = surplus - more
    return np.array([reach] + counts)


def ragged(rng, number_of, total, bound, skew):
    if number_of == 2:
        one = jax.random.randint(rng, (), max(1, total - bound), min(bound, total - 1) + 1)
        return jnp.stack([one, total - one])
    sizes = jnp.asarray(length_profile(number_of, total, bound, skew), jnp.int32)
    twos = (number_of - 1) // 2
    source_of, taker = sizes[1:1 + 2 * twos:2], sizes[2:2 + 2 * twos:2]
    room = jnp.minimum(source_of - 1, bound - taker)
    shifted = jax.random.randint(jax.random.fold_in(rng, 1), (twos,), 0, 1 << 20) % (room + 1)
    sizes = sizes.at[1:1 + 2 * twos:2].set(source_of - shifted).at[2:2 + 2 * twos:2].set(taker + shifted)
    return sizes[jax.random.permutation(jax.random.fold_in(rng, 2), number_of)]


def bell_draw(own_key, extent, width, limit, shards=(), kind=jnp.bfloat16):
    level = levels(own_key, extent, shards, -0.22, 0.18) if shards else 1.0
    values = jax.random.normal(own_key, extent, jnp.float32) * width * level
    return jnp.minimum(jnp.maximum(values, -limit), limit).astype(kind)


def gaussian_with(stream_key, extent, scale, reach, shards, heavy, held_as=jnp.bfloat16):
    array = scale * jax.random.normal(stream_key, extent, jnp.float32)
    if shards:
        array = array * levels(stream_key, extent, shards, -0.22, 0.18)
    return jnp.clip(strengthened(array, jax.random.fold_in(stream_key, 3), *heavy), -reach, reach).astype(held_as)


def setup_inputs(seed: int = 0) -> dict:
    key_of = jax.random.split(jax.random.key(seed), 11)
    return {
        "tokens": bell_draw(key_of[0], (TOKENS, DIN), 1.0, 6.0, ((0, 32),)),
        "block_modality": set_ends(jax.random.randint(key_of[1], (NBLK,), 0, MODES), jax.random.fold_in(key_of[1], 1), 0, MODES - 1).astype(jnp.int32),
        "live_blocks": ragged(key_of[2], N_SEQ, LIVE, BLK_DEV, 1).astype(jnp.int32),
        "mode_table": bell_draw(key_of[3], (MODES, DIN), 1.0, 5.0, (), jnp.float32),
        "latents": bell_draw(key_of[4], (LAT, DL), 1.0, 6.0, ((0, 32),)),
        "w_query": draw_w_query(jax.random.fold_in(key_of[10], 71), 0),
        "w_key": draw_w_key(jax.random.fold_in(key_of[10], 71), 0),
        "w_value": bell_draw(key_of[7], (DIN, DL), DIN ** -0.5, 0.1875, ((1, 8),)),
        "w_out": gaussian_with(key_of[8], (DL, DL), HD ** -0.5, 0.375, ((0, 8),), (0, 1, 8, 2.0)),
        "cotangent": bell_draw(key_of[9], (LAT, DL), 1.0, 6.0, ((0, 32),)),
    }


masked_floor = -1e+30

def normalize(values):
    mean = lax.optimization_barrier(jnp.mean(values, axis=-1, keepdims=True))
    centred = values - mean
    spread = lax.optimization_barrier(jnp.mean(centred * centred, axis=-1, keepdims=True))
    return centred * lax.rsqrt(spread + 1e-05)

def split_heads(matrix):
    return matrix.reshape(matrix.shape[0], HEADS, HD).transpose(1, 0, 2)

def join_heads(stack):
    return stack.transpose(1, 0, 2).reshape(stack.shape[1], HEADS * HD)

def reference(tokens, block_modality, live_blocks, mode_table, latents, w_query, w_key, w_value, w_out, cotangent):
    onehot = (block_modality[:, None] == jnp.arange(MODES, dtype=jnp.int32)[None, :]).astype(jnp.float32)
    block_embed = jnp.dot(onehot, mode_table, precision=lax.Precision.HIGHEST)
    shaped = tokens.astype(jnp.float32).reshape(NBLK, 128, DIN) + block_embed[:, None, :]
    normed = normalize(shaped.reshape(TOKENS, DIN)).astype(jnp.bfloat16)
    position = jnp.arange(TOKENS, dtype=jnp.int32)
    owner = position // TOK_DEV
    live = position % TOK_DEV < live_blocks[owner] * 128
    scale = HD ** (-0.5)
    lat_norm = normalize(latents.astype(jnp.float32)).astype(jnp.bfloat16)
    queries = jnp.dot(lat_norm, w_query, preferred_element_type=jnp.float32).astype(jnp.bfloat16)
    keys = jnp.dot(normed, w_key, preferred_element_type=jnp.float32).astype(jnp.bfloat16)
    values = jnp.dot(normed, w_value, preferred_element_type=jnp.float32).astype(jnp.bfloat16)

    def head_weights(query_h, key_h):
        scores = jnp.dot(query_h, key_h.T, preferred_element_type=jnp.float32) * scale
        scores = jnp.where(live[None, :], scores, masked_floor)
        top = lax.optimization_barrier(jnp.max(scores, axis=1))
        weights = jnp.exp(scores - top[:, None])
        return (weights, lax.optimization_barrier(jnp.sum(weights, axis=1)))

    def forward_head(operands):
        query_h, key_h, value_h = operands
        weights, totals = head_weights(query_h, key_h)
        summed = jnp.dot(weights.astype(jnp.bfloat16), value_h, preferred_element_type=jnp.float32)
        return ((summed / totals[:, None]).astype(jnp.bfloat16), totals)
    query_heads, key_heads, value_heads = (split_heads(queries), split_heads(keys), split_heads(values))
    attn_heads, totals_heads = lax.map(forward_head, (query_heads, key_heads, value_heads))
    attn = join_heads(attn_heads)
    mixed = (latents.astype(jnp.float32) + jnp.dot(attn, w_out, preferred_element_type=jnp.float32)).astype(jnp.bfloat16)
    back = jnp.dot(cotangent, w_out.T, preferred_element_type=jnp.float32).astype(jnp.bfloat16)

    def backward_head(operands):
        query_h, key_h, value_h, attn_h, back_h, totals = operands
        weights, unused = head_weights(query_h, key_h)
        delta = lax.optimization_barrier(jnp.sum(back_h.astype(jnp.float32) * attn_h.astype(jnp.float32), axis=1))
        dprob = jnp.dot(back_h, value_h.T, preferred_element_type=jnp.float32)
        dscore = (weights * (dprob - delta[:, None]) / totals[:, None] * scale).astype(jnp.bfloat16)
        normed_probs = (weights / totals[:, None]).astype(jnp.bfloat16)
        dvalue = jnp.dot(normed_probs.T, back_h, preferred_element_type=jnp.float32).astype(jnp.bfloat16)
        dkey = jnp.dot(dscore.T, query_h, preferred_element_type=jnp.float32).astype(jnp.bfloat16)
        return (dkey, dvalue)
    dkey_heads, dvalue_heads = lax.map(backward_head, (query_heads, key_heads, value_heads, attn_heads, split_heads(back), totals_heads))
    grad_key = jnp.dot(normed.T, join_heads(dkey_heads), preferred_element_type=jnp.float32)
    grad_value = jnp.dot(normed.T, join_heads(dvalue_heads), preferred_element_type=jnp.float32)
    return (mixed, grad_key, grad_value)
```

```python
import jax
import jax.numpy as jnp
from jax import lax
from jax.sharding import Mesh, PartitionSpec as P

HD = 512
SCALE = HD ** (-0.5)
FLOOR = -1e30
XY = ("x", "y")
SEQ = ("x", "y", "core")
f32 = jnp.float32
bf16 = jnp.bfloat16


def normalize(values):
    mean = jnp.mean(values, axis=-1, keepdims=True)
    centred = values - mean
    spread = jnp.mean(centred * centred, axis=-1, keepdims=True)
    return centred * lax.rsqrt(spread + 1e-05)


def spread_out(block, axes, count):
    return lax.all_to_all(
        jnp.broadcast_to(block[None], (count,) + block.shape), axes, 0, 0, tiled=True
    )


def on_device(
    tokens,
    block_modality,
    live_blocks,
    mode_table,
    latents,
    w_query,
    w_key,
    w_value,
    w_out,
    cotangent,
    *,
    chips,
    heads,
):
    tok_count, in_width = tokens.shape
    modes = mode_table.shape[0]
    width = w_key.shape[1]
    rows_here, lat_width = latents.shape
    lat_half = chips * rows_here
    swap = [(0, 1), (1, 0)]

    lat_norm = normalize(latents.astype(f32)).astype(bf16)
    query_rows = jnp.dot(lat_norm, w_query, preferred_element_type=f32).astype(bf16)
    back_rows = lax.dot_general(
        cotangent, w_out, (((1,), (1,)), ((), ())), preferred_element_type=f32
    ).astype(bf16)
    both = spread_out(jnp.concatenate([query_rows, back_rows], axis=1), XY, chips)
    both = both.reshape(lat_half, 2 * width)
    queries, back = both[:, :width], both[:, width:]

    onehot = (block_modality[:, None] == jnp.arange(modes, dtype=jnp.int32)[None, :]).astype(f32)
    block_embed = jnp.dot(onehot, mode_table, precision=lax.Precision.HIGHEST)
    shaped = tokens.astype(f32).reshape(tok_count // 128, 128, in_width) + block_embed[:, None, :]
    normed_own = normalize(shaped.reshape(tok_count, in_width)).astype(bf16)
    normed_other = lax.ppermute(normed_own, "core", swap)
    live_other = lax.ppermute(live_blocks, "core", swap)
    normed = jnp.concatenate([normed_own, normed_other], axis=0)
    place = jnp.arange(tok_count, dtype=jnp.int32)
    live = jnp.concatenate([place < live_blocks[0] * 128, place < live_other[0] * 128])
    keys = jnp.dot(normed, w_key, preferred_element_type=f32).astype(bf16)
    values = jnp.dot(normed, w_value, preferred_element_type=f32).astype(bf16)

    nt = (((1,), (1,)), ((), ()))
    tn = (((0,), (0,)), ((), ()))
    scores = lax.dot_general(queries, keys, nt, preferred_element_type=f32) * SCALE
    scores = jnp.where(live[None, :], scores, FLOOR)
    top = jnp.max(scores, axis=1)
    weights = jnp.exp(scores - top[:, None])
    total = jnp.sum(weights, axis=1)
    dprob = lax.dot_general(back, values, nt, preferred_element_type=f32)
    cross = jnp.sum(weights * dprob, axis=1)

    stats = spread_out(jnp.stack([top, total, cross]), XY, chips)
    tops, totals, crosses = stats[:, 0], stats[:, 1], stats[:, 2]
    top_all = jnp.max(tops, axis=0)
    factor = jnp.exp(tops - top_all)
    total_all = jnp.sum(factor * totals, axis=0)
    delta = jnp.sum(factor * crosses, axis=0) / total_all
    gain = jnp.exp(top - top_all) / total_all

    partial = jnp.dot(weights.astype(bf16), values, preferred_element_type=f32).astype(bf16)
    partials = lax.all_to_all(partial.reshape(chips, rows_here, width), XY, 0, 0, tiled=True)
    chip = lax.axis_index(XY)
    mine = lax.dynamic_slice_in_dim(factor, chip * rows_here, rows_here, 1)
    mine_total = lax.dynamic_slice_in_dim(total_all, chip * rows_here, rows_here, 0)
    attn_rows = (
        jnp.sum(partials.astype(f32) * mine[:, :, None], axis=0) / mine_total[:, None]
    ).astype(bf16)
    projected = jnp.dot(attn_rows, w_out, preferred_element_type=f32).astype(bf16)
    share = rows_here // heads
    pieces = lax.all_to_all(projected.reshape(heads, share, lat_width), "mp", 0, 0, tiled=True)
    head = lax.axis_index("mp")
    lat_share = lax.dynamic_slice_in_dim(latents, head * share, share, 0)
    mixed_share = (lat_share.astype(f32) + jnp.sum(pieces.astype(f32), axis=0)).astype(bf16)
    mixed = spread_out(mixed_share, "mp", heads).reshape(rows_here, lat_width)

    scaled = weights * gain[:, None]
    probs = scaled.astype(bf16)
    dscore = (scaled * (dprob - delta[:, None]) * SCALE).astype(bf16)
    dvalue = lax.dot_general(probs, back, tn, preferred_element_type=f32).astype(bf16)
    dkey = lax.dot_general(dscore, queries, tn, preferred_element_type=f32).astype(bf16)
    stacked = jnp.concatenate([dkey, dvalue], axis=1)
    grads = lax.dot_general(normed, stacked, tn, preferred_element_type=f32).astype(bf16)
    grads = grads.reshape(chips, 2, in_width // (2 * chips), 2 * width)
    core = lax.axis_index("core")
    keep = lax.dynamic_index_in_dim(grads, core, 1, keepdims=False)
    give = lax.dynamic_index_in_dim(grads, 1 - core, 1, keepdims=False)
    took = lax.ppermute(give, "core", swap)
    chip_grads = (keep.astype(f32) + took.astype(f32)).astype(bf16)
    parts = lax.all_to_all(chip_grads, XY, 0, 0, tiled=True)
    out = jnp.sum(parts.astype(f32), axis=0)
    return mixed, out[:, :width], out[:, width:]


def solution(mesh):
    seq, heads = mesh.devices.shape
    side = 4
    fine = Mesh(mesh.devices.reshape(seq // (2 * side), side, 2, heads), SEQ + ("mp",))

    def body(*args):
        return on_device(*args, chips=seq // 2, heads=heads)

    in_specs = (
        P(SEQ, None),
        P(SEQ),
        P(SEQ),
        P(),
        P(SEQ, None),
        P(None, "mp"),
        P(None, "mp"),
        P(None, "mp"),
        P("mp", None),
        P(SEQ, None),
    )
    out_specs = (P(SEQ, None), P(SEQ, "mp"), P(SEQ, "mp"))
    return jax.shard_map(
        body, mesh=fine, in_specs=in_specs, out_specs=out_specs, check_vma=False
    )
```

```python
import functools

import jax
import jax.numpy as jnp
from jax import lax
from jax.experimental import pallas as pl
from jax.experimental.pallas import tpu as pltpu
from jax.sharding import Mesh, PartitionSpec as P

HD = 512
SCALE = HD ** (-0.5)
FLOOR = -1e30
XY = ("x", "y")
SEQ = ("x", "y", "core")
f32 = jnp.float32
bf16 = jnp.bfloat16


def normalize(values):
    mean = jnp.mean(values, axis=-1, keepdims=True)
    centred = values - mean
    spread = jnp.mean(centred * centred, axis=-1, keepdims=True)
    return centred * lax.rsqrt(spread + 1e-05)


def spread_out(block, axes, count):
    return lax.all_to_all(
        jnp.broadcast_to(block[None], (count,) + block.shape), axes, 0, 0, tiled=True
    )


def dot_nn(a, b):
    return jnp.dot(a, b, preferred_element_type=f32)


def dot_nt(a, b):
    return lax.dot_general(a, b, (((1,), (1,)), ((), ())), preferred_element_type=f32)


def forward_kernel(live_ref, q_ref, b_ref, k_ref, v_ref, w_ref, d_ref, part_ref, stat_ref):
    rows = q_ref.shape[0]
    slots = k_ref.shape[0]
    half = slots // 2
    place = lax.broadcasted_iota(jnp.int32, (1, slots), 1)
    bound = jnp.where(place < half, live_ref[0] * 128, half + live_ref[1] * 128)
    live = place < bound
    step = rows // 2
    for start in range(0, rows, step):
        here = pl.ds(start, step)
        scores = dot_nt(q_ref[here, :], k_ref[...]) * SCALE
        scores = jnp.where(live, scores, FLOOR)
        top = jnp.max(scores, axis=1, keepdims=True)
        weights = jnp.exp(scores - top)
        total = jnp.sum(weights, axis=1, keepdims=True)
        dprob = dot_nt(b_ref[here, :], v_ref[...])
        cross = jnp.sum(weights * dprob, axis=1, keepdims=True)
        rounded = weights.astype(bf16)
        w_ref[here, :] = rounded
        d_ref[here, :] = dprob
        part_ref[here, :] = dot_nn(rounded, v_ref[...]).astype(bf16)
        lane = lax.broadcasted_iota(jnp.int32, (step, 128), 1)
        packed = jnp.where(lane == 0, top, jnp.where(lane == 1, total, cross))
        stat_ref[:, here] = packed.T[:8]


def forward(live, both, keys, values):
    lat, double = both.shape
    width = double // 2
    slots = keys.shape[0]
    rows = 256
    whole = lambda i: (0, 0)
    return pl.pallas_call(
        forward_kernel,
        grid=(lat // rows,),
        in_specs=[
            pl.BlockSpec(memory_space=pltpu.SMEM),
            pl.BlockSpec((rows, width), lambda i: (i, 0)),
            pl.BlockSpec((rows, width), lambda i: (i, 1)),
            pl.BlockSpec((slots, width), whole),
            pl.BlockSpec((slots, width), whole),
        ],
        out_specs=[
            pl.BlockSpec((rows, slots), lambda i: (i, 0)),
            pl.BlockSpec((rows, slots), lambda i: (i, 0)),
            pl.BlockSpec((rows, width), lambda i: (i, 0)),
            pl.BlockSpec((8, rows), lambda i: (0, i)),
        ],
        out_shape=[
            jax.ShapeDtypeStruct((lat, slots), bf16),
            jax.ShapeDtypeStruct((lat, slots), f32),
            jax.ShapeDtypeStruct((lat, width), bf16),
            jax.ShapeDtypeStruct((8, lat), f32),
        ],
        compiler_params=pltpu.CompilerParams(vmem_limit_bytes=40 << 20),
        cost_estimate=pl.CostEstimate(
            flops=6 * lat * slots * width,
            bytes_accessed=6 * lat * slots + 6 * lat * width + 4 * slots * width,
            transcendentals=lat * slots,
        ),
    )(live, both, both, keys, values)


def backward_kernel(stat_ref, own_ref, t_ref, w_ref, d_ref, n_ref, out_ref, scaled, delta, grads):
    step = pl.program_id(0)
    lat = stat_ref.shape[2]
    width = t_ref.shape[0] // 2
    block = w_ref.shape[1]

    @pl.when(step == 0)
    def _():
        tops, totals, crosses = stat_ref[:, 0, :], stat_ref[:, 1, :], stat_ref[:, 2, :]
        top = jnp.max(tops, axis=0, keepdims=True)
        factor = jnp.exp(tops - top)
        total = jnp.sum(factor * totals, axis=0, keepdims=True)
        mean = jnp.sum(factor * crosses, axis=0, keepdims=True) / total
        delta[...] = jnp.broadcast_to(mean, (128, lat)).T
        gain = jnp.exp(own_ref[0:1, :] - top) / total
        scaled[:width] = (t_ref[:width].astype(f32) * (gain * SCALE)).astype(bf16)
        scaled[width:] = (t_ref[width:].astype(f32) * gain).astype(bf16)

    for part in range(0, block, 128):
        here = pl.ds(part, 128)
        dscore = (w_ref[:, here].astype(f32) * (d_ref[:, here] - delta[...])).astype(bf16)
        there = pl.ds(pl.multiple_of(step * block + part, 128), 128)
        grads[:width, there] = dot_nn(scaled[:width], dscore).astype(bf16)
        grads[width:, there] = dot_nn(scaled[width:], w_ref[:, here]).astype(bf16)

    @pl.when(step == pl.num_programs(0) - 1)
    def _():
        size = out_ref.shape[0] // 4
        for row in range(0, out_ref.shape[0], size):
            out_ref[pl.ds(row, size), :] = dot_nt(n_ref[pl.ds(row, size), :], grads[...]).astype(bf16)


def backward(stats, own, turned, weights, dprob, normed_t):
    lat, slots = weights.shape
    double = turned.shape[0]
    in_width = normed_t.shape[0]
    block = 256
    return pl.pallas_call(
        backward_kernel,
        grid=(slots // block,),
        in_specs=[
            pl.BlockSpec(stats.shape, lambda i: (0, 0, 0)),
            pl.BlockSpec(own.shape, lambda i: (0, 0)),
            pl.BlockSpec(turned.shape, lambda i: (0, 0)),
            pl.BlockSpec((lat, block), lambda i: (0, i)),
            pl.BlockSpec((lat, block), lambda i: (0, i)),
            pl.BlockSpec(normed_t.shape, lambda i: (0, 0)),
        ],
        out_specs=pl.BlockSpec((in_width, double), lambda i: (0, 0)),
        out_shape=jax.ShapeDtypeStruct((in_width, double), bf16),
        scratch_shapes=[
            pltpu.VMEM((double, lat), bf16),
            pltpu.VMEM((lat, 128), f32),
            pltpu.VMEM((double, slots), bf16),
        ],
        compiler_params=pltpu.CompilerParams(vmem_limit_bytes=40 << 20),
        cost_estimate=pl.CostEstimate(
            flops=2 * slots * double * (lat + in_width),
            bytes_accessed=6 * lat * slots + 2 * in_width * (slots + double) + 2 * double * lat,
            transcendentals=lat,
        ),
    )(stats, own, turned, weights, dprob, normed_t)


def on_device(
    tokens,
    block_modality,
    live_blocks,
    mode_table,
    latents,
    w_query,
    w_key,
    w_value,
    w_out,
    cotangent,
    *,
    chips,
    heads,
):
    tok_count, in_width = tokens.shape
    modes = mode_table.shape[0]
    width = w_key.shape[1]
    rows_here, lat_width = latents.shape
    lat_half = chips * rows_here
    swap = [(0, 1), (1, 0)]

    lat_norm = normalize(latents.astype(f32)).astype(bf16)
    query_rows = jnp.dot(lat_norm, w_query, preferred_element_type=f32).astype(bf16)
    back_rows = lax.dot_general(
        cotangent, w_out, (((1,), (1,)), ((), ())), preferred_element_type=f32
    ).astype(bf16)
    both = spread_out(jnp.concatenate([query_rows, back_rows], axis=1), XY, chips)
    both = both.reshape(lat_half, 2 * width)

    onehot = (block_modality[:, None] == jnp.arange(modes, dtype=jnp.int32)[None, :]).astype(f32)
    block_embed = jnp.dot(onehot, mode_table, precision=lax.Precision.HIGHEST)
    shaped = tokens.astype(f32).reshape(tok_count // 128, 128, in_width) + block_embed[:, None, :]
    normed_own = normalize(shaped.reshape(tok_count, in_width)).astype(bf16)
    normed_other = lax.ppermute(normed_own, "core", swap)
    live_other = lax.ppermute(live_blocks, "core", swap)
    normed = jnp.concatenate([normed_own, normed_other], axis=0)
    live = jnp.concatenate([live_blocks, live_other])
    keys = jnp.dot(normed, w_key, preferred_element_type=f32).astype(bf16)
    values = jnp.dot(normed, w_value, preferred_element_type=f32).astype(bf16)

    core = lax.axis_index("core")
    turned_tokens = normed.T.reshape(chips, 2, in_width // (2 * chips), 2 * tok_count)
    turned_tokens = jnp.concatenate(
        [lax.dynamic_index_in_dim(turned_tokens, c, 1, keepdims=False) for c in (core, 1 - core)]
    ).reshape(in_width, 2 * tok_count)

    weights, dprob, partial, own = forward(live, both, keys, values)
    stats = spread_out(own, XY, chips)
    factor = jnp.exp(stats[:, 0] - jnp.max(stats[:, 0], axis=0))
    total_all = jnp.sum(factor * stats[:, 1], axis=0)

    partials = lax.all_to_all(partial.reshape(chips, rows_here, width), XY, 0, 0, tiled=True)
    chip = lax.axis_index(XY)
    mine = lax.dynamic_slice_in_dim(factor, chip * rows_here, rows_here, 1)
    mine_total = lax.dynamic_slice_in_dim(total_all, chip * rows_here, rows_here, 0)
    attn_rows = (
        jnp.sum(partials.astype(f32) * mine[:, :, None], axis=0) / mine_total[:, None]
    ).astype(bf16)
    projected = jnp.dot(attn_rows, w_out, preferred_element_type=f32).astype(bf16)
    share = rows_here // heads
    pieces = lax.all_to_all(projected.reshape(heads, share, lat_width), "mp", 0, 0, tiled=True)
    head = lax.axis_index("mp")
    lat_share = lax.dynamic_slice_in_dim(latents, head * share, share, 0)
    mixed_share = (lat_share.astype(f32) + jnp.sum(pieces.astype(f32), axis=0)).astype(bf16)
    mixed = spread_out(mixed_share, "mp", heads).reshape(rows_here, lat_width)

    grads = backward(stats, own, both.T, weights, dprob, turned_tokens)
    grads = grads.reshape(2, chips, in_width // (2 * chips), 2 * width)
    keep, give = grads[0], grads[1]
    took = lax.ppermute(give, "core", swap)
    chip_grads = (keep.astype(f32) + took.astype(f32)).astype(bf16)
    parts = lax.all_to_all(chip_grads, XY, 0, 0, tiled=True)
    out = jnp.sum(parts.astype(f32), axis=0)
    return mixed, out[:, :width], out[:, width:]


def solution(mesh):
    seq, heads = mesh.devices.shape
    side = 4
    fine = Mesh(mesh.devices.reshape(seq // (2 * side), side, 2, heads), SEQ + ("mp",))

    def body(*args):
        return on_device(*args, chips=seq // 2, heads=heads)

    in_specs = (
        P(SEQ, None),
        P(SEQ),
        P(SEQ),
        P(),
        P(SEQ, None),
        P(None, "mp"),
        P(None, "mp"),
        P(None, "mp"),
        P("mp", None),
        P(SEQ, None),
    )
    out_specs = (P(SEQ, None), P(SEQ, "mp"), P(SEQ, "mp"))
    return jax.shard_map(
        body, mesh=fine, in_specs=in_specs, out_specs=out_specs, check_vma=False
    )
```

```python
import functools

import jax
import jax.numpy as jnp
from jax import lax
from jax.experimental import pallas as pl
from jax.experimental.pallas import tpu as pltpu
from jax.sharding import Mesh, PartitionSpec as P

HD = 512
SCALE = HD ** (-0.5)
FLOOR = -1e30
XY = ("x", "y")
SEQ = ("x", "y", "core")
f32 = jnp.float32
bf16 = jnp.bfloat16


def normalize(values):
    mean = jnp.mean(values, axis=-1, keepdims=True)
    centred = values - mean
    spread = jnp.mean(centred * centred, axis=-1, keepdims=True)
    return centred * lax.rsqrt(spread + 1e-05)


def spread_out(block, axes, count):
    return lax.all_to_all(
        jnp.broadcast_to(block[None], (count,) + block.shape), axes, 0, 0, tiled=True
    )


def ring_gather(block, axis):
    count = lax.axis_size(axis)
    return jnp.stack(
        [block]
        + [
            lax.ppermute(block, axis, [(i, (i + k) % count) for i in range(count)])
            for k in range(1, count)
        ]
    )


def cube_gather(block, axis):
    count = lax.axis_size(axis)
    me = lax.axis_index(axis)
    out = block[None]
    far = count // 2
    while far:
        other = lax.ppermute(out, axis, [(i, i ^ far) for i in range(count)])
        upper = (me & far) != 0
        out = jnp.stack(
            [jnp.where(upper, other, out), jnp.where(upper, out, other)], axis=1
        ).reshape((2 * out.shape[0],) + block.shape)
        far //= 2
    return out


def dot_nn(a, b):
    return jnp.dot(a, b, preferred_element_type=f32)


def dot_nt(a, b):
    return lax.dot_general(a, b, (((1,), (1,)), ((), ())), preferred_element_type=f32)


def dot_tn(a, b):
    return lax.dot_general(a, b, (((0,), (0,)), ((), ())), preferred_element_type=f32)


def far(*arrays):
    return [pltpu.with_memory_space_constraint(a, pltpu.HBM) for a in arrays]


def limits(bytes_wanted):
    return pltpu.CompilerParams(vmem_limit_bytes=bytes_wanted)


def query_kernel(lat_ref, w_ref, out_ref, normed, total):
    step = pl.program_id(0)
    chunk = w_ref.shape[0]

    @pl.when(step == 0)
    def _():
        normed[...] = normalize(lat_ref[...].astype(f32)).astype(bf16)
        total[...] = jnp.zeros_like(total)

    columns = pl.ds(pl.multiple_of(step * chunk, chunk), chunk)
    total[...] += dot_nn(normed[:, columns], w_ref[...])

    @pl.when(step == pl.num_programs(0) - 1)
    def _():
        result = total[...].astype(bf16)
        for copy in range(out_ref.shape[0]):
            out_ref[copy] = result


def make_queries(latents, w_query, copies):
    rows, depth = latents.shape
    width = w_query.shape[1]
    steps = 4
    return pl.pallas_call(
        query_kernel,
        grid=(steps,),
        in_specs=[
            pl.BlockSpec((rows, depth), lambda i: (0, 0)),
            pl.BlockSpec((depth // steps, width), lambda i: (i, 0)),
        ],
        out_specs=pl.BlockSpec((copies, rows, width), lambda i: (0, 0, 0)),
        out_shape=jax.ShapeDtypeStruct((copies, rows, width), bf16),
        scratch_shapes=[pltpu.VMEM((rows, depth), bf16), pltpu.VMEM((rows, width), f32)],
        compiler_params=limits(16 << 20),
        cost_estimate=pl.CostEstimate(
            flops=2 * rows * depth * width,
            bytes_accessed=2 * (rows + width) * depth + 2 * copies * rows * width,
            transcendentals=rows,
        ),
    )(*far(latents, w_query))


def back_kernel(cot_ref, w_ref, after_ref, out_ref, total):
    step = pl.program_id(0)

    @pl.when(step == 0)
    def _():
        total[...] = jnp.zeros_like(total)

    total[...] += dot_nt(cot_ref[...], w_ref[...])

    @pl.when(step == pl.num_programs(0) - 1)
    def _():
        out_ref[...] = total[...].astype(bf16)


def make_back(cotangent, w_out, after):
    rows, depth = cotangent.shape
    width = w_out.shape[0]
    steps = 4
    return pl.pallas_call(
        back_kernel,
        grid=(steps,),
        in_specs=[
            pl.BlockSpec((rows, depth // steps), lambda i: (0, i)),
            pl.BlockSpec((width, depth // steps), lambda i: (0, i)),
            pl.BlockSpec(memory_space=pl.ANY),
        ],
        out_specs=pl.BlockSpec((rows, width), lambda i: (0, 0)),
        out_shape=jax.ShapeDtypeStruct((rows, width), bf16),
        scratch_shapes=[pltpu.VMEM((rows, width), f32)],
        compiler_params=limits(16 << 20),
        cost_estimate=pl.CostEstimate(
            flops=2 * rows * depth * width,
            bytes_accessed=2 * (rows + width) * depth,
            transcendentals=0,
        ),
    )(*far(cotangent, w_out), after)


def token_kernel(
    facts_ref, table_ref, own_ref, other_ref, wk_ref, wv_ref, after_ref, k_ref, v_ref, n_ref
):
    def work(side, ref):
        for block in range(ref.shape[0] // 128):
            mode = facts_ref[side, block]
            place = pl.ds(block * 128, 128)
            raw = ref[place, :].astype(f32) + table_ref[pl.ds(mode, 1), :]
            n_ref[place, :] = normalize(raw).astype(bf16)

    @pl.when(pl.program_id(0) == 0)
    def _():
        work(0, own_ref)

    @pl.when(pl.program_id(0) == 1)
    def _():
        work(1, other_ref)

    k_ref[...] = dot_nn(n_ref[...], wk_ref[...]).astype(bf16)
    v_ref[...] = dot_nn(n_ref[...], wv_ref[...]).astype(bf16)


def make_tokens(facts, table, own, other, w_key, w_value, after):
    slots, in_width = own.shape
    width = w_key.shape[1]
    whole = lambda i: (0, 0)
    side = lambda i: (i, 0)
    return pl.pallas_call(
        token_kernel,
        grid=(2,),
        in_specs=[pl.BlockSpec(memory_space=pltpu.SMEM)]
        + [pl.BlockSpec(a.shape, whole) for a in (table, own, other, w_key, w_value)]
        + [pl.BlockSpec(memory_space=pl.ANY)],
        out_specs=[
            pl.BlockSpec((slots, width), side),
            pl.BlockSpec((slots, width), side),
            pl.BlockSpec((slots, in_width), side),
        ],
        out_shape=[
            pltpu.HBM((2 * slots, width), bf16),
            pltpu.HBM((2 * slots, width), bf16),
            pltpu.HBM((2 * slots, in_width), bf16),
        ],
        compiler_params=limits(40 << 20),
        cost_estimate=pl.CostEstimate(
            flops=8 * slots * in_width * width,
            bytes_accessed=4 * in_width * (2 * slots + width) + 8 * slots * width,
            transcendentals=2 * slots,
        ),
    )(facts, table, *far(own), other, *far(w_key, w_value), after)


def in_three(value):
    high = value.astype(bf16).astype(f32)
    middle = (value - high).astype(bf16).astype(f32)
    return high, middle, value - high - middle


def scores_kernel(facts_ref, q_ref, k_ref, v_ref, w_ref, part_ref, top_ref):
    rows, width = q_ref.shape
    slots = k_ref.shape[0]
    half = slots // 2
    last = facts_ref.shape[1] - 1
    place = lax.broadcasted_iota(jnp.int32, (1, slots), 1)
    bound = jnp.where(place < half, facts_ref[0, last] * 128, half + facts_ref[1, last] * 128)
    scores = dot_nt(q_ref[...], k_ref[...]) * SCALE
    scores = jnp.where(place < bound, scores, FLOOR)
    top = jnp.max(scores, axis=1, keepdims=True)
    weights = jnp.exp(scores - top)
    total = jnp.sum(weights, axis=1, keepdims=True)
    rounded = weights.astype(bf16)
    w_ref[...] = rounded
    part_ref[:, :width] = dot_nn(rounded, v_ref[...]).astype(bf16)
    lane = lax.broadcasted_iota(jnp.int32, (rows, 128), 1)
    packed = jnp.zeros((rows, 128), f32)
    for index, term in enumerate(in_three(top) + in_three(total)):
        packed = jnp.where(lane == index, term, packed)
    part_ref[:, width:] = packed.astype(bf16)
    top_ref[...] = jnp.broadcast_to(top, (rows, 128))


def attend(facts, queries, keys, values):
    lat, width = queries.shape
    slots = keys.shape[0]
    rows = 256
    whole = lambda i: (0, 0)
    return pl.pallas_call(
        scores_kernel,
        grid=(lat // rows,),
        in_specs=[
            pl.BlockSpec(memory_space=pltpu.SMEM),
            pl.BlockSpec((rows, width), lambda i: (i, 0)),
            pl.BlockSpec((slots, width), whole),
            pl.BlockSpec((slots, width), whole),
        ],
        out_specs=[
            pl.BlockSpec((rows, slots), lambda i: (i, 0)),
            pl.BlockSpec((rows, width + 128), lambda i: (i, 0)),
            pl.BlockSpec((rows, 128), lambda i: (i, 0)),
        ],
        out_shape=[
            pltpu.HBM((lat, slots), bf16),
            pltpu.HBM((lat, width + 128), bf16),
            pltpu.HBM((lat, 128), f32),
        ],
        compiler_params=limits(32 << 20),
        cost_estimate=pl.CostEstimate(
            flops=4 * lat * slots * width,
            bytes_accessed=2 * lat * slots + 6 * lat * width + 4 * slots * width,
            transcendentals=lat * slots,
        ),
    )(facts, queries, *far(keys, values))


def combine_kernel(part_ref, back_ref, near_ref, attn_ref, stat_ref, passed_ref):
    passed_ref[...] = near_ref[...]
    rows, width = back_ref.shape
    terms = part_ref[:, :, width:].astype(f32)
    tops = terms[:, :, 0:1] + terms[:, :, 1:2] + terms[:, :, 2:3]
    totals = terms[:, :, 3:4] + terms[:, :, 4:5] + terms[:, :, 5:6]
    top = jnp.max(tops, axis=0)
    factors = jnp.exp(tops - top[None])
    total = jnp.sum(factors * totals, axis=0)
    summed = jnp.sum(part_ref[:, :, :width].astype(f32) * factors, axis=0)
    attn = (summed / total).astype(bf16)
    attn_ref[...] = attn
    delta = jnp.sum(back_ref[...].astype(f32) * attn.astype(f32), axis=1, keepdims=True)
    lane = lax.broadcasted_iota(jnp.int32, (rows, 128), 1)
    packed = jnp.where(lane == 0, top, jnp.where(lane == 1, total, delta))
    stat_ref[...] = jnp.concatenate([packed, packed], axis=0).T[:8]


def combine(partials, back, near):
    rows, width = back.shape
    vmem = pl.BlockSpec(memory_space=pltpu.VMEM)
    return pl.pallas_call(
        combine_kernel,
        in_specs=[vmem] * 3,
        out_specs=[vmem] * 3,
        out_shape=[
            jax.ShapeDtypeStruct((rows, width), bf16),
            jax.ShapeDtypeStruct((8, 2 * rows), f32),
            jax.ShapeDtypeStruct(near.shape, bf16),
        ],
        compiler_params=limits(24 << 20),
        cost_estimate=pl.CostEstimate(
            flops=2 * partials.size, bytes_accessed=2 * partials.size, transcendentals=rows
        ),
    )(partials, back, near)


def chip_entry(place_ref, chip, side_x, side_y):
    back_x = lax.rem(place_ref[0] - chip // side_y + side_x, side_x)
    back_y = lax.rem(place_ref[1] - chip % side_y + side_y, side_y)
    return back_x, back_y


def product_kernel(place_ref, b_ref, v_ref, d_ref, rows_ref):
    side_x, side_y, rows = b_ref.shape[:3]
    step = pl.program_id(0)
    for row in range(side_y):
        entry = chip_entry(place_ref, step * side_y + row, side_x, side_y)
        rows_ref[pl.ds(row * rows, rows), :] = b_ref[entry]
    d_ref[...] = dot_nt(rows_ref[...], v_ref[...])


def products(place, back_rings, values):
    side_x, side_y, rows, width = back_rings.shape
    lat = side_x * side_y * rows
    slots = values.shape[0]
    block = side_y * rows
    return pl.pallas_call(
        product_kernel,
        grid=(side_x,),
        in_specs=[
            pl.BlockSpec(memory_space=pltpu.SMEM),
            pl.BlockSpec(back_rings.shape, lambda i: (0, 0, 0, 0)),
            pl.BlockSpec((slots, width), lambda i: (0, 0)),
        ],
        out_specs=[
            pl.BlockSpec((block, slots), lambda i: (i, 0)),
            pl.BlockSpec((block, width), lambda i: (i, 0)),
        ],
        out_shape=[pltpu.HBM((lat, slots), f32), pltpu.HBM((lat, width), bf16)],
        compiler_params=limits(24 << 20),
        cost_estimate=pl.CostEstimate(
            flops=2 * lat * slots * width,
            bytes_accessed=4 * lat * slots + 2 * width * (2 * lat + slots),
            transcendentals=0,
        ),
    )(place, back_rings, *far(values))


def backward_kernel(
    place_ref, stat_ref, top_ref, q_ref, b_ref, w_ref, d_ref, out_ref, scaled, delta
):
    width = q_ref.shape[1]
    block = w_ref.shape[1]
    side_x, side_y = stat_ref.shape[0], stat_ref.shape[1]
    rows = stat_ref.shape[3] // 2

    @pl.when(pl.program_id(0) == 0)
    def _():
        for chip in range(side_x * side_y):
            piece = stat_ref[chip_entry(place_ref, chip, side_x, side_y)]
            turned = jnp.concatenate([piece] * 16, axis=0).T[:rows]
            here = pl.ds(chip * rows, rows)
            gain = jnp.exp(top_ref[here, :] - turned[:, 0:1]) / turned[:, 1:2]
            delta[here, :] = jnp.broadcast_to(turned[:, 2:3], (rows, 128))
            gain = jnp.concatenate([gain] * (width // 128), axis=1)
            scaled[here, :width] = (q_ref[here, :].astype(f32) * (gain * SCALE)).astype(bf16)
            scaled[here, width:] = (b_ref[here, :].astype(f32) * gain).astype(bf16)

    mean = jnp.concatenate([delta[...]] * (block // 128), axis=1)
    dscore = (w_ref[...].astype(f32) * (d_ref[...] - mean)).astype(bf16)
    out_ref[:, :width] = dot_tn(dscore, scaled[:, :width]).astype(bf16)
    out_ref[:, width:] = dot_tn(w_ref[...], scaled[:, width:]).astype(bf16)


def backward(place, stats, tops, queries, back, weights, dprob):
    lat, slots = weights.shape
    width = queries.shape[1]
    block = 256
    whole = lambda i: (0, 0)
    return pl.pallas_call(
        backward_kernel,
        grid=(slots // block,),
        in_specs=[
            pl.BlockSpec(memory_space=pltpu.SMEM),
            pl.BlockSpec(stats.shape, lambda i: (0, 0, 0, 0)),
            pl.BlockSpec(tops.shape, whole),
            pl.BlockSpec(queries.shape, whole),
            pl.BlockSpec(back.shape, whole),
            pl.BlockSpec((lat, block), lambda i: (0, i)),
            pl.BlockSpec((lat, block), lambda i: (0, i)),
        ],
        out_specs=pl.BlockSpec((block, 2 * width), lambda i: (i, 0)),
        out_shape=pltpu.HBM((slots, 2 * width), bf16),
        scratch_shapes=[pltpu.VMEM((lat, 2 * width), bf16), pltpu.VMEM((lat, 128), f32)],
        compiler_params=limits(32 << 20),
        cost_estimate=pl.CostEstimate(
            flops=4 * slots * width * lat,
            bytes_accessed=6 * lat * slots + 4 * slots * width + 4 * width * lat,
            transcendentals=lat,
        ),
    )(place, stats, tops, queries, *far(back, weights, dprob))


def weight_kernel(place_ref, n_ref, g_ref, after_ref, keep_ref, give_ref):
    result = dot_tn(n_ref[...], g_ref[...]).astype(bf16)
    chips, share = keep_ref.shape[0], keep_ref.shape[1]
    for core, refs in ((0, (keep_ref, give_ref)), (1, (give_ref, keep_ref))):

        @pl.when(place_ref[2] == core)
        def _():
            for chip in range(chips):
                for part in range(2):
                    first = (2 * chip + part) * share
                    refs[part][chip] = result[first : first + share, :]


def weight_grads(place, normed, grads, after, chips):
    slots, in_width = normed.shape
    double = grads.shape[1]
    share = in_width // (2 * chips)
    steps = 4
    piece = jax.ShapeDtypeStruct((chips, share, double), bf16)
    piece_spec = pl.BlockSpec((chips // steps, share, double), lambda i: (i, 0, 0))
    return pl.pallas_call(
        weight_kernel,
        grid=(steps,),
        in_specs=[
            pl.BlockSpec(memory_space=pltpu.SMEM),
            pl.BlockSpec((slots, in_width // steps), lambda i: (0, i)),
            pl.BlockSpec((slots, double), lambda i: (0, 0)),
            pl.BlockSpec(memory_space=pl.ANY),
        ],
        out_specs=[piece_spec] * 2,
        out_shape=[piece] * 2,
        compiler_params=limits(32 << 20),
        cost_estimate=pl.CostEstimate(
            flops=2 * slots * double * in_width,
            bytes_accessed=2 * (slots * (in_width + double) + in_width * double),
            transcendentals=0,
        ),
    )(place, *far(normed, grads), after)


def add_kernel(pieces_ref, lat_ref, out_ref):
    total = lat_ref[...].astype(f32) + jnp.sum(pieces_ref[...].astype(f32), axis=0)
    out_ref[...] = total.astype(bf16)


def add_pieces(pieces, latents):
    vmem = pl.BlockSpec(memory_space=pltpu.VMEM)
    return pl.pallas_call(
        add_kernel,
        in_specs=[vmem, vmem],
        out_specs=vmem,
        out_shape=jax.ShapeDtypeStruct(latents.shape, bf16),
        cost_estimate=pl.CostEstimate(
            flops=pieces.size, bytes_accessed=2 * pieces.size, transcendentals=0
        ),
    )(pieces, latents)


def on_device(
    tokens,
    block_modality,
    live_blocks,
    mode_table,
    latents,
    w_query,
    w_key,
    w_value,
    w_out,
    cotangent,
    *,
    chips,
    heads,
):
    tok_count, in_width = tokens.shape
    width = w_key.shape[1]
    rows_here, lat_width = latents.shape
    lat_half = chips * rows_here
    swap = [(0, 1), (1, 0)]

    tokens_other = lax.ppermute(tokens, "core", swap)
    facts_own = jnp.concatenate([block_modality, live_blocks])
    facts = jnp.stack([facts_own, lax.ppermute(facts_own, "core", swap)])

    query_copies = make_queries(latents, w_query, chips)
    queries = lax.all_to_all(query_copies, XY, 0, 0, tiled=True).reshape(lat_half, width)
    keys, values, normed = make_tokens(
        facts, mode_table, tokens, tokens_other, w_key, w_value, query_copies
    )

    weights, partial, tops = attend(facts, queries, keys, values)
    partials = lax.all_to_all(
        partial.reshape(chips, rows_here, width + 128), XY, 0, 0, tiled=True
    )
    back_rows = make_back(cotangent, w_out, tops)
    attn_rows, stat_rows, back_near = combine(partials, back_rows, ring_gather(back_rows, "y"))
    stats = ring_gather(ring_gather(stat_rows, "y"), "x")
    back_rings = ring_gather(back_near, "x")
    projected = jnp.dot(attn_rows, w_out, preferred_element_type=f32).astype(bf16)
    share = rows_here // heads
    pieces = lax.all_to_all(projected.reshape(heads, share, lat_width), "mp", 0, 0, tiled=True)

    place = jnp.stack([lax.axis_index(axis) for axis in ("x", "y", "core")]).astype(jnp.int32)
    dprob, back = products(place, back_rings, values)
    grads = backward(place, stats, tops, queries, back, weights, dprob)

    head = lax.axis_index("mp")
    lat_share = lax.dynamic_slice_in_dim(latents, head * share, share, 0)
    mixed_share = add_pieces(pieces, lat_share)
    mixed = cube_gather(mixed_share, "mp").reshape(rows_here, lat_width)
    keep, give = weight_grads(place, normed, grads, mixed_share, chips)
    took = lax.ppermute(give, "core", swap)
    chip_grads = (keep.astype(f32) + took.astype(f32)).astype(bf16)
    parts = lax.all_to_all(chip_grads, XY, 0, 0, tiled=True)
    out = jnp.sum(parts.astype(f32), axis=0)
    return mixed, out[:, :width], out[:, width:]


def solution(mesh):
    seq, heads = mesh.devices.shape
    side = 4
    fine = Mesh(mesh.devices.reshape(seq // (2 * side), side, 2, heads), SEQ + ("mp",))

    def body(*args):
        return on_device(*args, chips=seq // 2, heads=heads)

    in_specs = (
        P(SEQ, None),
        P(SEQ),
        P(SEQ),
        P(),
        P(SEQ, None),
        P(None, "mp"),
        P(None, "mp"),
        P(None, "mp"),
        P("mp", None),
        P(SEQ, None),
    )
    out_specs = (P(SEQ, None), P(SEQ, "mp"), P(SEQ, "mp"))
    return jax.shard_map(
        body, mesh=fine, in_specs=in_specs, out_specs=out_specs, check_vma=False
    )
```

```python
import functools

import jax
import jax.numpy as jnp
from jax import lax
from jax.experimental import pallas as pl
from jax.experimental.pallas import tpu as pltpu
from jax.sharding import Mesh, PartitionSpec as P

HD = 512
SCALE = HD ** (-0.5)
FLOOR = -1e30
XY = ("x", "y")
SEQ = ("x", "y", "core")
f32 = jnp.float32
bf16 = jnp.bfloat16


def normalize(values):
    mean = jnp.mean(values, axis=-1, keepdims=True)
    centred = values - mean
    spread = jnp.mean(centred * centred, axis=-1, keepdims=True)
    return centred * lax.rsqrt(spread + 1e-05)


def spread_out(block, axes, count):
    return lax.all_to_all(
        jnp.broadcast_to(block[None], (count,) + block.shape), axes, 0, 0, tiled=True
    )


def ring_blocks(block, axis):
    count = lax.axis_size(axis)
    return [block] + [
        lax.ppermute(block, axis, [(i, (i + k) % count) for i in range(count)])
        for k in range(1, count)
    ]


def ring_gather(block, axis):
    return jnp.stack(ring_blocks(block, axis))


def dot_nn(a, b):
    return jnp.dot(a, b, preferred_element_type=f32)


def dot_nt(a, b):
    return lax.dot_general(a, b, (((1,), (1,)), ((), ())), preferred_element_type=f32)


def dot_tn(a, b):
    return lax.dot_general(a, b, (((0,), (0,)), ((), ())), preferred_element_type=f32)


def far(*arrays):
    return [pltpu.with_memory_space_constraint(a, pltpu.HBM) for a in arrays]


def limits(bytes_wanted):
    return pltpu.CompilerParams(vmem_limit_bytes=bytes_wanted)


def latent_kernel(lat_ref, wq_ref, cot_ref, wo_ref, q_ref, b_ref, normed, total_q, total_b):
    step = pl.program_id(0)
    chunk = wq_ref.shape[0]

    @pl.when(step == 0)
    def _():
        normed[...] = normalize(lat_ref[...].astype(f32)).astype(bf16)
        total_q[...] = jnp.zeros_like(total_q)
        total_b[...] = jnp.zeros_like(total_b)

    columns = pl.ds(pl.multiple_of(step * chunk, chunk), chunk)
    total_q[...] += dot_nn(normed[:, columns], wq_ref[...])
    total_b[...] += dot_nt(cot_ref[...], wo_ref[...])

    @pl.when(step == pl.num_programs(0) - 1)
    def _():
        q_ref[...] = total_q[...].astype(bf16)
        b_ref[...] = total_b[...].astype(bf16)


def make_latents(latents, w_query, cotangent, w_out):
    rows, depth = latents.shape
    width = w_query.shape[1]
    steps = 4
    out = jax.ShapeDtypeStruct((rows, width), bf16)
    return pl.pallas_call(
        latent_kernel,
        grid=(steps,),
        in_specs=[
            pl.BlockSpec((rows, depth), lambda i: (0, 0)),
            pl.BlockSpec((depth // steps, width), lambda i: (i, 0)),
            pl.BlockSpec((rows, depth // steps), lambda i: (0, i)),
            pl.BlockSpec((width, depth // steps), lambda i: (0, i)),
        ],
        out_specs=[pl.BlockSpec((rows, width), lambda i: (0, 0))] * 2,
        out_shape=[out, out],
        scratch_shapes=[
            pltpu.VMEM((rows, depth), bf16),
            pltpu.VMEM((rows, width), f32),
            pltpu.VMEM((rows, width), f32),
        ],
        compiler_params=limits(24 << 20),
        cost_estimate=pl.CostEstimate(
            flops=4 * rows * depth * width,
            bytes_accessed=4 * (rows + width) * depth,
            transcendentals=rows,
        ),
    )(*far(latents, w_query, cotangent, w_out))


def token_kernel(
    facts_ref, table_ref, own_ref, other_ref, wk_ref, wv_ref, after_ref, k_ref, v_ref, n_ref
):
    def work(side, ref):
        for block in range(ref.shape[0] // 128):
            mode = facts_ref[side, block]
            place = pl.ds(block * 128, 128)
            raw = ref[place, :].astype(f32) + table_ref[pl.ds(mode, 1), :]
            n_ref[place, :] = normalize(raw).astype(bf16)

    @pl.when(pl.program_id(0) == 0)
    def _():
        work(0, own_ref)

    @pl.when(pl.program_id(0) == 1)
    def _():
        work(1, other_ref)

    k_ref[...] = dot_nn(n_ref[...], wk_ref[...]).astype(bf16)
    v_ref[...] = dot_nn(n_ref[...], wv_ref[...]).astype(bf16)


def make_tokens(facts, table, own, other, w_key, w_value, after):
    slots, in_width = own.shape
    width = w_key.shape[1]
    whole = lambda i: (0, 0)
    side = lambda i: (i, 0)
    return pl.pallas_call(
        token_kernel,
        grid=(2,),
        in_specs=[pl.BlockSpec(memory_space=pltpu.SMEM)]
        + [pl.BlockSpec(a.shape, whole) for a in (table, own, other, w_key, w_value)]
        + [pl.BlockSpec(memory_space=pl.ANY)],
        out_specs=[
            pl.BlockSpec((slots, width), side),
            pl.BlockSpec((slots, width), side),
            pl.BlockSpec((slots, in_width), side),
        ],
        out_shape=[
            pltpu.HBM((2 * slots, width), bf16),
            pltpu.HBM((2 * slots, width), bf16),
            pltpu.HBM((2 * slots, in_width), bf16),
        ],
        compiler_params=limits(40 << 20),
        cost_estimate=pl.CostEstimate(
            flops=8 * slots * in_width * width,
            bytes_accessed=4 * in_width * (2 * slots + width) + 8 * slots * width,
            transcendentals=2 * slots,
        ),
    )(facts, table, *far(own), other, *far(w_key, w_value), after)


def pass_kernel(array_ref, after_ref, out_ref):
    del array_ref, after_ref, out_ref


def pass_on(array, after):
    hbm = pl.BlockSpec(memory_space=pl.ANY)
    return pl.pallas_call(
        pass_kernel,
        in_specs=[hbm, hbm],
        out_specs=hbm,
        out_shape=jax.ShapeDtypeStruct(array.shape, array.dtype),
        input_output_aliases={0: 0},
    )(array, after)


def in_three(value):
    high = value.astype(bf16).astype(f32)
    middle = (value - high).astype(bf16).astype(f32)
    return high, middle, value - high - middle


def gathered(refs, here, rows):
    side_far, side_near = len(refs), refs[0].shape[0]
    for back_far, ref in enumerate(refs):
        for back_near in range(side_near):
            at_far = lax.rem(here[0] - back_far + side_far, side_far)
            at_near = lax.rem(here[1] - back_near + side_near, side_near)
            yield at_far, at_near, ref[back_near]


def scores_kernel(
    facts_ref, place_ref, q0_ref, q1_ref, q2_ref, q3_ref, b0_ref, b1_ref, b2_ref, b3_ref, k_ref,
    v_ref, w_ref, d_ref, part_ref, stat_ref, both_ref, ordered
):
    rows = w_ref.shape[0]
    slots, width = k_ref.shape
    share = q0_ref.shape[1]
    half = slots // 2
    last = facts_ref.shape[1] - 1
    step = pl.program_id(0)

    @pl.when(step == 0)
    def _():
        at_x, at_y = place_ref[0], place_ref[1]
        side = q0_ref.shape[0]
        for x, y, block in gathered((q0_ref, q1_ref, q2_ref, q3_ref), (at_x, at_y), share):
            first = pl.multiple_of((x * side + y) * share, share)
            ordered[pl.ds(first, share), :width] = block
        for y, x, block in gathered((b0_ref, b1_ref, b2_ref, b3_ref), (at_y, at_x), share):
            first = pl.multiple_of((x * side + y) * share, share)
            ordered[pl.ds(first, share), width:] = block

    taken = ordered[pl.ds(pl.multiple_of(step * rows, rows), rows), :]
    both_ref[...] = taken
    place = lax.broadcasted_iota(jnp.int32, (1, slots), 1)
    bound = jnp.where(place < half, facts_ref[0, last] * 128, half + facts_ref[1, last] * 128)
    scores = dot_nt(taken[:, :width], k_ref[...]) * SCALE
    scores = jnp.where(place < bound, scores, FLOOR)
    top = jnp.max(scores, axis=1, keepdims=True)
    weights = jnp.exp(scores - top)
    total = jnp.sum(weights, axis=1, keepdims=True)
    rounded = weights.astype(bf16)
    w_ref[...] = rounded
    dprob = dot_nt(taken[:, width:], v_ref[...])
    d_ref[...] = dprob
    cross = jnp.sum(weights * dprob, axis=1, keepdims=True)
    part_ref[:, :width] = dot_nn(rounded, v_ref[...]).astype(bf16)
    lane = lax.broadcasted_iota(jnp.int32, (rows, 128), 1)
    packed = jnp.zeros((rows, 128), f32)
    for index, term in enumerate(in_three(top) + in_three(total)):
        packed = jnp.where(lane == index, term, packed)
    part_ref[:, width:] = packed.astype(bf16)
    stat_ref[...] = jnp.where(lane == 0, top, jnp.where(lane == 1, total, cross)).T[:8]


def attend(facts, place, query_rings, back_rings, keys, values):
    side, share, width = query_rings[0].shape
    lat = len(query_rings) * side * share
    slots = keys.shape[0]
    rows = 256
    whole = lambda i: (0, 0)
    chunk = lambda i: (i, 0)
    smem = pl.BlockSpec(memory_space=pltpu.SMEM)
    ring = pl.BlockSpec((side, share, width), lambda i: (0, 0, 0))
    return pl.pallas_call(
        scores_kernel,
        grid=(lat // rows,),
        in_specs=[smem, smem] + [ring] * 8 + [pl.BlockSpec((slots, width), whole)] * 2,
        out_specs=[
            pl.BlockSpec((rows, slots), chunk),
            pl.BlockSpec((rows, slots), chunk),
            pl.BlockSpec((rows, width + 128), chunk),
            pl.BlockSpec((8, rows), lambda i: (0, i)),
            pl.BlockSpec((rows, 2 * width), chunk),
        ],
        out_shape=[
            pltpu.HBM((lat, slots), bf16),
            pltpu.HBM((lat, slots), f32),
            pltpu.HBM((lat, width + 128), bf16),
            jax.ShapeDtypeStruct((8, lat), f32),
            pltpu.HBM((lat, 2 * width), bf16),
        ],
        scratch_shapes=[pltpu.VMEM((lat, 2 * width), bf16)],
        compiler_params=limits(40 << 20),
        cost_estimate=pl.CostEstimate(
            flops=6 * lat * slots * width,
            bytes_accessed=6 * lat * slots + 10 * lat * width + 4 * slots * width,
            transcendentals=lat * slots,
        ),
    )(facts, place, *query_rings, *back_rings, *far(keys, values))


def combine_kernel(part_ref, after_ref, attn_ref):
    width = attn_ref.shape[1]
    terms = part_ref[:, :, width:].astype(f32)
    tops = terms[:, :, 0:1] + terms[:, :, 1:2] + terms[:, :, 2:3]
    totals = terms[:, :, 3:4] + terms[:, :, 4:5] + terms[:, :, 5:6]
    top = jnp.max(tops, axis=0)
    factors = jnp.exp(tops - top[None])
    total = jnp.sum(factors * totals, axis=0)
    summed = jnp.sum(part_ref[:, :, :width].astype(f32) * factors, axis=0)
    attn_ref[...] = (summed / total).astype(bf16)


def combine(partials, after):
    _, rows, wide = partials.shape
    vmem = pl.BlockSpec(memory_space=pltpu.VMEM)
    return pl.pallas_call(
        combine_kernel,
        in_specs=[vmem, pl.BlockSpec(memory_space=pl.ANY)],
        out_specs=vmem,
        out_shape=jax.ShapeDtypeStruct((rows, wide - 128), bf16),
        compiler_params=limits(24 << 20),
        cost_estimate=pl.CostEstimate(
            flops=2 * partials.size, bytes_accessed=2 * partials.size, transcendentals=rows
        ),
    )(partials, after)


def backward_kernel(
    core_ref, stat_ref, own_ref, both_ref, w_ref, d_ref, n_ref, after_ref, keep_ref,
    give_ref,    scaled, delta, grads, normed, result, arrived
):
    step = pl.program_id(0)
    width = both_ref.shape[1] // 2
    block = w_ref.shape[1]
    lat = both_ref.shape[0]
    fetch = pltpu.make_async_copy(n_ref, normed, arrived)

    @pl.when(step == 0)
    def _():
        fetch.start()
        every = stat_ref[...]
        count = every.shape[1] - 2
        tops = jnp.max(every[:, :count], axis=1)
        totals, crosses = every[:, count], every[:, count + 1]
        top = jnp.max(tops, axis=0, keepdims=True)
        factor = jnp.exp(tops - top)
        total = jnp.sum(factor * totals, axis=0, keepdims=True)
        mean = jnp.sum(factor * crosses, axis=0, keepdims=True) / total
        delta[...] = jnp.broadcast_to(mean, (128, lat)).T
        gain = jnp.exp(own_ref[0:1, :] - top) / total
        gain = jnp.broadcast_to(gain, (128, lat)).T
        gain = jnp.concatenate([gain] * (width // 128), axis=1)
        scaled[:, :width] = (both_ref[:, :width].astype(f32) * (gain * SCALE)).astype(bf16)
        scaled[:, width:] = (both_ref[:, width:].astype(f32) * gain).astype(bf16)

    mean = jnp.concatenate([delta[...]] * (block // 128), axis=1)
    dscore = (w_ref[...].astype(f32) * (d_ref[...] - mean)).astype(bf16)
    there = pl.ds(pl.multiple_of(step * block, block), block)
    grads[there, :width] = dot_tn(dscore, scaled[:, :width]).astype(bf16)
    grads[there, width:] = dot_tn(w_ref[...], scaled[:, width:]).astype(bf16)

    @pl.when(step == pl.num_programs(0) - 1)
    def _():
        fetch.wait()
        result[...] = dot_tn(normed[...], grads[...]).astype(bf16)
        chips, share = keep_ref.shape[0], keep_ref.shape[1]
        for core, refs in ((0, (keep_ref, give_ref)), (1, (give_ref, keep_ref))):

            @pl.when(core_ref[0] == core)
            def _():
                for chip in range(chips):
                    for part in range(2):
                        rows = pl.ds((2 * chip + part) * share, share)
                        refs[part][chip] = result[rows, :]


def backward(core, stats, own, both, weights, dprob, normed, after, chips):
    lat, slots = weights.shape
    width = both.shape[1] // 2
    in_width = normed.shape[1]
    share = in_width // (2 * chips)
    block = 256
    whole = lambda i: (0, 0)
    piece = pltpu.HBM((chips, share, 2 * width), bf16)
    piece_spec = pl.BlockSpec((chips, share, 2 * width), lambda i: (0, 0, 0))
    return pl.pallas_call(
        backward_kernel,
        grid=(slots // block,),
        in_specs=[
            pl.BlockSpec(memory_space=pltpu.SMEM),
            pl.BlockSpec(stats.shape, lambda i: (0, 0, 0)),
            pl.BlockSpec(own.shape, whole),
            pl.BlockSpec(both.shape, whole),
            pl.BlockSpec((lat, block), lambda i: (0, i)),
            pl.BlockSpec((lat, block), lambda i: (0, i)),
            pl.BlockSpec(memory_space=pl.ANY),
            pl.BlockSpec(memory_space=pl.ANY),
        ],
        out_specs=[piece_spec] * 2,
        out_shape=[piece] * 2,
        scratch_shapes=[
            pltpu.VMEM((lat, 2 * width), bf16),
            pltpu.VMEM((lat, 128), f32),
            pltpu.VMEM((slots, 2 * width), bf16),
            pltpu.VMEM(normed.shape, bf16),
            pltpu.VMEM((in_width, 2 * width), bf16),
            pltpu.SemaphoreType.DMA,
        ],
        compiler_params=limits(40 << 20),
        cost_estimate=pl.CostEstimate(
            flops=4 * slots * width * (lat + in_width),
            bytes_accessed=6 * lat * slots + 2 * in_width * (slots + 2 * width) + 4 * width * lat,
            transcendentals=lat,
        ),
    )(core, stats, own, *far(both, weights, dprob, normed), after)


def add_kernel(pieces_ref, lat_ref, after_ref, out_ref):
    total = lat_ref[...].astype(f32) + jnp.sum(pieces_ref[...].astype(f32), axis=0)
    out_ref[...] = total.astype(bf16)


def add_pieces(pieces, latents, after):
    vmem = pl.BlockSpec(memory_space=pltpu.VMEM)
    return pl.pallas_call(
        add_kernel,
        in_specs=[vmem, vmem, pl.BlockSpec(memory_space=pl.ANY)],
        out_specs=vmem,
        out_shape=jax.ShapeDtypeStruct(latents.shape, bf16),
        cost_estimate=pl.CostEstimate(
            flops=pieces.size, bytes_accessed=2 * pieces.size, transcendentals=0
        ),
    )(pieces, latents, after)


def place_kernel(low_ref, v0_ref, v1_ref, v2_ref, v3_ref, out_ref):
    refs = (v0_ref, v1_ref, v2_ref, v3_ref)
    low = low_ref[0]
    for move, ref in enumerate(refs):
        at = jnp.where(move & 1, 1 - low % 2, low % 2) + 2 * jnp.where(
            move & 2, 1 - low // 2, low // 2
        )
        for high in range(ref.shape[0]):
            out_ref[high * len(refs) + at] = ref[high]


def place_pieces(low, pieces):
    pair, rows, width = pieces[0].shape
    vmem = pl.BlockSpec(memory_space=pltpu.VMEM)
    shape = (pair * len(pieces), rows, width)
    return pl.pallas_call(
        place_kernel,
        in_specs=[pl.BlockSpec(memory_space=pltpu.SMEM)] + [vmem] * len(pieces),
        out_specs=vmem,
        out_shape=jax.ShapeDtypeStruct(shape, bf16),
        compiler_params=limits(16 << 20),
        cost_estimate=pl.CostEstimate(
            flops=0, bytes_accessed=4 * pair * len(pieces) * rows * width, transcendentals=0
        ),
    )(low, *pieces)


def on_device(
    tokens,
    block_modality,
    live_blocks,
    mode_table,
    latents,
    w_query,
    w_key,
    w_value,
    w_out,
    cotangent,
    *,
    chips,
    heads,
):
    tok_count, in_width = tokens.shape
    width = w_key.shape[1]
    rows_here, lat_width = latents.shape
    lat_half = chips * rows_here
    swap = [(0, 1), (1, 0)]

    tokens_other = lax.ppermute(tokens, "core", swap)
    facts_own = jnp.concatenate([block_modality, live_blocks])
    facts = jnp.stack([facts_own, lax.ppermute(facts_own, "core", swap)])

    query_rows, back_rows = make_latents(latents, w_query, cotangent, w_out)
    query_rings = ring_blocks(ring_gather(query_rows, "y"), "x")
    back_rings = ring_blocks(ring_gather(back_rows, "x"), "y")
    keys, values, normed = make_tokens(
        facts, mode_table, tokens, tokens_other, w_key, w_value, query_rows
    )

    place = jnp.stack([lax.axis_index(axis) for axis in ("x", "y", "core")]).astype(jnp.int32)
    weights, dprob, partial, own, both = attend(
        facts, place, query_rings, back_rings, keys, values
    )

    near = ring_gather(own[:3], "y")
    near_tops = near[:, 0]
    scale = jnp.exp(near_tops - jnp.max(near_tops, axis=0))
    near_sums = jnp.sum(near[:, 1:] * scale[:, None], axis=0)
    stats = ring_gather(jnp.concatenate([near_tops, near_sums]), "x")

    partials = lax.all_to_all(
        partial.reshape(chips, rows_here, width + 128), XY, 0, 0, tiled=True
    )
    share = rows_here // heads
    lat_share = lax.dynamic_slice_in_dim(latents, lax.axis_index("mp") * share, share, 0)
    attn_rows = combine(partials, lat_share)
    projected = jnp.dot(attn_rows, w_out, preferred_element_type=f32).astype(bf16)
    pieces = lax.all_to_all(projected.reshape(heads, share, lat_width), "mp", 0, 0, tiled=True)
    core = lax.axis_index("core")[None].astype(jnp.int32)
    keep, give = backward(core, stats, own, both, weights, dprob, normed, projected, chips)

    took = lax.ppermute(pass_on(give, pieces), "core", swap)
    mixed_share = add_pieces(pieces, lat_share, give)
    chip_grads = (keep.astype(f32) + took.astype(f32)).astype(bf16)
    head = lax.axis_index("mp")
    across = lax.ppermute(mixed_share, "mp", [(i, i ^ 4) for i in range(heads)])
    upper = head >= 4
    pair = jnp.stack(
        [jnp.where(upper, across, mixed_share), jnp.where(upper, mixed_share, across)]
    )
    quads = [pair] + [
        lax.ppermute(pair, "mp", [(i, i ^ move) for i in range(heads)]) for move in (1, 2, 3)
    ]
    mixed = place_pieces((head % 4)[None].astype(jnp.int32), quads).reshape(rows_here, lat_width)
    parts = lax.all_to_all(chip_grads, XY, 0, 0, tiled=True)
    out = jnp.sum(parts.astype(f32), axis=0)
    return mixed, out[:, :width], out[:, width:]


def solution(mesh):
    seq, heads = mesh.devices.shape
    side = 4
    fine = Mesh(mesh.devices.reshape(seq // (2 * side), side, 2, heads), SEQ + ("mp",))

    def body(*args):
        return on_device(*args, chips=seq // 2, heads=heads)

    in_specs = (
        P(SEQ, None),
        P(SEQ),
        P(SEQ),
        P(),
        P(SEQ, None),
        P(None, "mp"),
        P(None, "mp"),
        P(None, "mp"),
        P("mp", None),
        P(SEQ, None),
    )
    out_specs = (P(SEQ, None), P(SEQ, "mp"), P(SEQ, "mp"))
    return jax.shard_map(
        body, mesh=fine, in_specs=in_specs, out_specs=out_specs, check_vma=False
    )
```

```python
import functools

import jax
import jax.numpy as jnp
from jax import lax
from jax.experimental import pallas as pl
from jax.experimental.pallas import tpu as pltpu
from jax.sharding import Mesh, PartitionSpec as P

HD = 512
SCALE = HD ** (-0.5)
FLOOR = -1e30
XY = ("x", "y")
SEQ = ("x", "y", "core")
f32 = jnp.float32
bf16 = jnp.bfloat16


def normalize(values):
    mean = jnp.mean(values, axis=-1, keepdims=True)
    centred = values - mean
    spread = jnp.mean(centred * centred, axis=-1, keepdims=True)
    return centred * lax.rsqrt(spread + 1e-05)


def spread_out(block, axes, count):
    return lax.all_to_all(
        jnp.broadcast_to(block[None], (count,) + block.shape), axes, 0, 0, tiled=True
    )


def ring_blocks(block, axis):
    count = lax.axis_size(axis)
    return [block] + [
        lax.ppermute(block, axis, [(i, (i + k) % count) for i in range(count)])
        for k in range(1, count)
    ]


def ring_gather(block, axis):
    return jnp.stack(ring_blocks(block, axis))


def dot_nn(a, b):
    return jnp.dot(a, b, preferred_element_type=f32)


def dot_nt(a, b):
    return lax.dot_general(a, b, (((1,), (1,)), ((), ())), preferred_element_type=f32)


def dot_tn(a, b):
    return lax.dot_general(a, b, (((0,), (0,)), ((), ())), preferred_element_type=f32)


def far(*arrays):
    return [pltpu.with_memory_space_constraint(a, pltpu.HBM) for a in arrays]


def limits(bytes_wanted):
    return pltpu.CompilerParams(vmem_limit_bytes=bytes_wanted)


def latent_kernel(lat_ref, wq_ref, cot_ref, wo_ref, q_ref, b_ref, normed, total_q, total_b):
    step = pl.program_id(0)
    chunk = wq_ref.shape[0]

    @pl.when(step == 0)
    def _():
        normed[...] = normalize(lat_ref[...].astype(f32)).astype(bf16)
        total_q[...] = jnp.zeros_like(total_q)
        total_b[...] = jnp.zeros_like(total_b)

    columns = pl.ds(pl.multiple_of(step * chunk, chunk), chunk)
    total_q[...] += dot_nn(normed[:, columns], wq_ref[...])
    total_b[...] += dot_nt(cot_ref[...], wo_ref[...])

    @pl.when(step == pl.num_programs(0) - 1)
    def _():
        q_ref[...] = total_q[...].astype(bf16)
        b_ref[...] = total_b[...].astype(bf16)


def make_latents(latents, w_query, cotangent, w_out):
    rows, depth = latents.shape
    width = w_query.shape[1]
    steps = 2
    out = jax.ShapeDtypeStruct((rows, width), bf16)
    return pl.pallas_call(
        latent_kernel,
        grid=(steps,),
        in_specs=[
            pl.BlockSpec((rows, depth), lambda i: (0, 0)),
            pl.BlockSpec((depth // steps, width), lambda i: (i, 0)),
            pl.BlockSpec((rows, depth // steps), lambda i: (0, i)),
            pl.BlockSpec((width, depth // steps), lambda i: (0, i)),
        ],
        out_specs=[pl.BlockSpec((rows, width), lambda i: (0, 0))] * 2,
        out_shape=[out, out],
        scratch_shapes=[
            pltpu.VMEM((rows, depth), bf16),
            pltpu.VMEM((rows, width), f32),
            pltpu.VMEM((rows, width), f32),
        ],
        compiler_params=limits(32 << 20),
        cost_estimate=pl.CostEstimate(
            flops=4 * rows * depth * width,
            bytes_accessed=4 * (rows + width) * depth,
            transcendentals=rows,
        ),
    )(*far(latents, w_query, cotangent, w_out))


def token_kernel(
    facts_ref, table_ref, own_ref, other_ref, wk_ref, wv_ref, after_ref, k_ref, v_ref, n_ref
):
    def work(side, ref):
        for block in range(ref.shape[0] // 128):
            mode = facts_ref[side, block]
            place = pl.ds(block * 128, 128)
            raw = ref[place, :].astype(f32) + table_ref[pl.ds(mode, 1), :]
            n_ref[place, :] = normalize(raw).astype(bf16)

    @pl.when(pl.program_id(0) == 0)
    def _():
        work(0, own_ref)

    @pl.when(pl.program_id(0) == 1)
    def _():
        work(1, other_ref)

    k_ref[...] = dot_nn(n_ref[...], wk_ref[...]).astype(bf16)
    v_ref[...] = dot_nn(n_ref[...], wv_ref[...]).astype(bf16)


def make_tokens(facts, table, own, other, w_key, w_value, after):
    slots, in_width = own.shape
    width = w_key.shape[1]
    whole = lambda i: (0, 0)
    side = lambda i: (i, 0)
    return pl.pallas_call(
        token_kernel,
        grid=(2,),
        in_specs=[pl.BlockSpec(memory_space=pltpu.SMEM)]
        + [pl.BlockSpec(a.shape, whole) for a in (table, own, other, w_key, w_value)]
        + [pl.BlockSpec(memory_space=pl.ANY)],
        out_specs=[
            pl.BlockSpec((slots, width), side),
            pl.BlockSpec((slots, width), side),
            pl.BlockSpec((slots, in_width), side),
        ],
        out_shape=[
            pltpu.HBM((2 * slots, width), bf16),
            pltpu.HBM((2 * slots, width), bf16),
            pltpu.HBM((2 * slots, in_width), bf16),
        ],
        compiler_params=limits(40 << 20),
        cost_estimate=pl.CostEstimate(
            flops=8 * slots * in_width * width,
            bytes_accessed=4 * in_width * (2 * slots + width) + 8 * slots * width,
            transcendentals=2 * slots,
        ),
    )(facts, table, *far(own), other, *far(w_key, w_value), after)


def pass_kernel(array_ref, after_ref, out_ref):
    del array_ref, after_ref, out_ref


def pass_on(array, after):
    hbm = pl.BlockSpec(memory_space=pl.ANY)
    return pl.pallas_call(
        pass_kernel,
        in_specs=[hbm, hbm],
        out_specs=hbm,
        out_shape=jax.ShapeDtypeStruct(array.shape, array.dtype),
        input_output_aliases={0: 0},
    )(array, after)


def gathered(refs, here, rows):
    side_far, side_near = len(refs), refs[0].shape[0]
    for back_far, ref in enumerate(refs):
        for back_near in range(side_near):
            at_far = lax.rem(here[0] - back_far + side_far, side_far)
            at_near = lax.rem(here[1] - back_near + side_near, side_near)
            yield at_far, at_near, ref[back_near]


def scores_kernel(
    facts_ref, place_ref, q0_ref, q1_ref, q2_ref, q3_ref, b0_ref, b1_ref, b2_ref, b3_ref, k_ref,
    v_ref, w_ref, d_ref, part_ref, stat_ref, both_ref, ordered
):
    rows = w_ref.shape[0]
    slots, width = k_ref.shape
    share = q0_ref.shape[1]
    half = slots // 2
    last = facts_ref.shape[1] - 1
    step = pl.program_id(0)

    @pl.when(step == 0)
    def _():
        at_x, at_y = place_ref[0], place_ref[1]
        side = q0_ref.shape[0]
        for x, y, block in gathered((q0_ref, q1_ref, q2_ref, q3_ref), (at_x, at_y), share):
            first = pl.multiple_of((x * side + y) * share, share)
            ordered[pl.ds(first, share), :width] = block
        for y, x, block in gathered((b0_ref, b1_ref, b2_ref, b3_ref), (at_y, at_x), share):
            first = pl.multiple_of((x * side + y) * share, share)
            ordered[pl.ds(first, share), width:] = block

    taken = ordered[pl.ds(pl.multiple_of(step * rows, rows), rows), :]
    both_ref[...] = taken
    place = lax.broadcasted_iota(jnp.int32, (1, slots), 1)
    bound = jnp.where(place < half, facts_ref[0, last] * 128, half + facts_ref[1, last] * 128)
    scores = dot_nt(taken[:, :width], k_ref[...]) * SCALE
    scores = jnp.where(place < bound, scores, FLOOR)
    top = jnp.max(scores, axis=1, keepdims=True)
    weights = jnp.exp(scores - top)
    total = jnp.sum(weights, axis=1, keepdims=True)
    rounded = weights.astype(bf16)
    w_ref[...] = rounded
    dprob = dot_nt(taken[:, width:], v_ref[...])
    d_ref[...] = dprob
    cross = jnp.sum(weights * dprob, axis=1, keepdims=True)
    part_ref[...] = dot_nn(rounded, v_ref[...]).astype(bf16)
    lane = lax.broadcasted_iota(jnp.int32, (rows, 128), 1)
    stat_ref[...] = jnp.where(lane == 0, top, jnp.where(lane == 1, total, cross)).T[:8]


def attend(facts, place, query_rings, back_rings, keys, values):
    side, share, width = query_rings[0].shape
    lat = len(query_rings) * side * share
    slots = keys.shape[0]
    rows = 512
    whole = lambda i: (0, 0)
    chunk = lambda i: (i, 0)
    smem = pl.BlockSpec(memory_space=pltpu.SMEM)
    ring = pl.BlockSpec((side, share, width), lambda i: (0, 0, 0))
    return pl.pallas_call(
        scores_kernel,
        grid=(lat // rows,),
        in_specs=[smem, smem] + [ring] * 8 + [pl.BlockSpec((slots, width), whole)] * 2,
        out_specs=[
            pl.BlockSpec((rows, slots), chunk),
            pl.BlockSpec((rows, slots), chunk),
            pl.BlockSpec((rows, width), chunk),
            pl.BlockSpec((8, rows), lambda i: (0, i)),
            pl.BlockSpec((rows, 2 * width), chunk),
        ],
        out_shape=[
            pltpu.HBM((lat, slots), bf16),
            pltpu.HBM((lat, slots), f32),
            pltpu.HBM((lat, width), bf16),
            jax.ShapeDtypeStruct((8, lat), f32),
            pltpu.HBM((lat, 2 * width), bf16),
        ],
        scratch_shapes=[pltpu.VMEM((lat, 2 * width), bf16)],
        compiler_params=limits(48 << 20),
        cost_estimate=pl.CostEstimate(
            flops=6 * lat * slots * width,
            bytes_accessed=6 * lat * slots + 10 * lat * width + 4 * slots * width,
            transcendentals=lat * slots,
        ),
    )(facts, place, *query_rings, *back_rings, *far(keys, values))


def combine_kernel(place_ref, part_ref, stat_ref, after_ref, attn_ref):
    rows, width = attn_ref.shape
    side, lat = stat_ref.shape[0], stat_ref.shape[2]
    count = stat_ref.shape[1] - 2
    first = (place_ref[0] * count + place_ref[1]) * rows
    every = jnp.concatenate([stat_ref[back] for back in range(side)], axis=0)
    mine = pltpu.roll(every, lax.rem(lat - first, lat), 1)[:, :128]
    filler = jnp.zeros((128 - mine.shape[0], 128), f32)
    columns = jnp.concatenate([mine, filler], axis=0).T[:rows]
    stride = count + 2
    tops = [
        [columns[:, stride * x + y : stride * x + y + 1] for y in range(count)] for x in range(side)
    ]
    near = [functools.reduce(jnp.maximum, of_x) for of_x in tops]
    top = functools.reduce(jnp.maximum, near)
    total = jnp.zeros((rows, 1), f32)
    for x in range(side):
        at = stride * x + count
        total += jnp.exp(near[x] - top) * columns[:, at : at + 1]
    summed = jnp.zeros((rows, width), f32)
    for x in range(side):
        for y in range(count):
            at_x = lax.rem(place_ref[0] - x + side, side)
            at_y = lax.rem(place_ref[1] - y + count, count)
            part = part_ref[at_x * count + at_y].astype(f32)
            summed += part * jnp.exp(tops[x][y] - top)
    attn_ref[...] = (summed / total).astype(bf16)


def combine(place, partials, stats, after):
    _, rows, width = partials.shape
    vmem = pl.BlockSpec(memory_space=pltpu.VMEM)
    return pl.pallas_call(
        combine_kernel,
        in_specs=[
            pl.BlockSpec(memory_space=pltpu.SMEM),
            vmem,
            vmem,
            pl.BlockSpec(memory_space=pl.ANY),
        ],
        out_specs=vmem,
        out_shape=jax.ShapeDtypeStruct((rows, width), bf16),
        compiler_params=limits(24 << 20),
        cost_estimate=pl.CostEstimate(
            flops=2 * partials.size, bytes_accessed=2 * partials.size, transcendentals=rows
        ),
    )(place, partials, stats, after)


def backward_kernel(
    core_ref, stat_ref, own_ref, both_ref, w_ref, d_ref, n_ref, after_ref, keep_ref,
    give_ref,    scaled, delta, grads, normed, result, arrived
):
    step = pl.program_id(0)
    width = both_ref.shape[1] // 2
    block = w_ref.shape[1]
    lat = both_ref.shape[0]
    fetch = pltpu.make_async_copy(n_ref, normed, arrived)

    @pl.when(step == 0)
    def _():
        fetch.start()
        every = stat_ref[...]
        count = every.shape[1] - 2
        tops = jnp.max(every[:, :count], axis=1)
        totals, crosses = every[:, count], every[:, count + 1]
        top = jnp.max(tops, axis=0, keepdims=True)
        factor = jnp.exp(tops - top)
        total = jnp.sum(factor * totals, axis=0, keepdims=True)
        mean = jnp.sum(factor * crosses, axis=0, keepdims=True) / total
        delta[...] = jnp.broadcast_to(mean, (128, lat)).T
        gain = jnp.exp(own_ref[0:1, :] - top) / total
        gain = jnp.broadcast_to(gain, (128, lat)).T
        gain = jnp.concatenate([gain] * (width // 128), axis=1)
        scaled[:, :width] = (both_ref[:, :width].astype(f32) * (gain * SCALE)).astype(bf16)
        scaled[:, width:] = (both_ref[:, width:].astype(f32) * gain).astype(bf16)

    mean = jnp.concatenate([delta[...]] * (block // 128), axis=1)
    dscore = (w_ref[...].astype(f32) * (d_ref[...] - mean)).astype(bf16)
    there = pl.ds(pl.multiple_of(step * block, block), block)
    grads[there, :width] = dot_tn(dscore, scaled[:, :width]).astype(bf16)
    grads[there, width:] = dot_tn(w_ref[...], scaled[:, width:]).astype(bf16)

    @pl.when(step == pl.num_programs(0) - 1)
    def _():
        fetch.wait()
        result[...] = dot_tn(normed[...], grads[...]).astype(bf16)
        chips, share = keep_ref.shape[0], keep_ref.shape[1]
        for core, refs in ((0, (keep_ref, give_ref)), (1, (give_ref, keep_ref))):

            @pl.when(core_ref[0] == core)
            def _():
                for chip in range(chips):
                    for part in range(2):
                        rows = pl.ds((2 * chip + part) * share, share)
                        refs[part][chip] = result[rows, :]


def backward(core, stats, own, both, weights, dprob, normed, after, chips):
    lat, slots = weights.shape
    width = both.shape[1] // 2
    in_width = normed.shape[1]
    share = in_width // (2 * chips)
    block = 256
    whole = lambda i: (0, 0)
    piece = pltpu.HBM((chips, share, 2 * width), bf16)
    piece_spec = pl.BlockSpec((chips, share, 2 * width), lambda i: (0, 0, 0))
    return pl.pallas_call(
        backward_kernel,
        grid=(slots // block,),
        in_specs=[
            pl.BlockSpec(memory_space=pltpu.SMEM),
            pl.BlockSpec(stats.shape, lambda i: (0, 0, 0)),
            pl.BlockSpec(own.shape, whole),
            pl.BlockSpec(both.shape, whole),
            pl.BlockSpec((lat, block), lambda i: (0, i)),
            pl.BlockSpec((lat, block), lambda i: (0, i)),
            pl.BlockSpec(memory_space=pl.ANY),
            pl.BlockSpec(memory_space=pl.ANY),
        ],
        out_specs=[piece_spec] * 2,
        out_shape=[piece] * 2,
        scratch_shapes=[
            pltpu.VMEM((lat, 2 * width), bf16),
            pltpu.VMEM((lat, 128), f32),
            pltpu.VMEM((slots, 2 * width), bf16),
            pltpu.VMEM(normed.shape, bf16),
            pltpu.VMEM((in_width, 2 * width), bf16),
            pltpu.SemaphoreType.DMA,
        ],
        compiler_params=limits(40 << 20),
        cost_estimate=pl.CostEstimate(
            flops=4 * slots * width * (lat + in_width),
            bytes_accessed=6 * lat * slots + 2 * in_width * (slots + 2 * width) + 4 * width * lat,
            transcendentals=lat,
        ),
    )(core, stats, own, *far(both, weights, dprob, normed), after)


def add_kernel(pieces_ref, lat_ref, after_ref, out_ref):
    total = lat_ref[...].astype(f32) + jnp.sum(pieces_ref[...].astype(f32), axis=0)
    out_ref[...] = total.astype(bf16)


def add_pieces(pieces, latents, after):
    vmem = pl.BlockSpec(memory_space=pltpu.VMEM)
    return pl.pallas_call(
        add_kernel,
        in_specs=[vmem, vmem, pl.BlockSpec(memory_space=pl.ANY)],
        out_specs=vmem,
        out_shape=jax.ShapeDtypeStruct(latents.shape, bf16),
        cost_estimate=pl.CostEstimate(
            flops=pieces.size, bytes_accessed=2 * pieces.size, transcendentals=0
        ),
    )(pieces, latents, after)


def place_kernel(low_ref, v0_ref, v1_ref, v2_ref, v3_ref, out_ref):
    refs = (v0_ref, v1_ref, v2_ref, v3_ref)
    low = low_ref[0]
    for move, ref in enumerate(refs):
        at = jnp.where(move & 1, 1 - low % 2, low % 2) + 2 * jnp.where(
            move & 2, 1 - low // 2, low // 2
        )
        for high in range(ref.shape[0]):
            out_ref[high * len(refs) + at] = ref[high]


def place_pieces(low, pieces):
    pair, rows, width = pieces[0].shape
    vmem = pl.BlockSpec(memory_space=pltpu.VMEM)
    shape = (pair * len(pieces), rows, width)
    return pl.pallas_call(
        place_kernel,
        in_specs=[pl.BlockSpec(memory_space=pltpu.SMEM)] + [vmem] * len(pieces),
        out_specs=vmem,
        out_shape=jax.ShapeDtypeStruct(shape, bf16),
        compiler_params=limits(16 << 20),
        cost_estimate=pl.CostEstimate(
            flops=0, bytes_accessed=4 * pair * len(pieces) * rows * width, transcendentals=0
        ),
    )(low, *pieces)


def on_device(
    tokens,
    block_modality,
    live_blocks,
    mode_table,
    latents,
    w_query,
    w_key,
    w_value,
    w_out,
    cotangent,
    *,
    chips,
    heads,
):
    tok_count, in_width = tokens.shape
    width = w_key.shape[1]
    rows_here, lat_width = latents.shape
    lat_half = chips * rows_here
    swap = [(0, 1), (1, 0)]

    tokens_other = lax.ppermute(tokens, "core", swap)
    facts_own = jnp.concatenate([block_modality, live_blocks])
    facts = jnp.stack([facts_own, lax.ppermute(facts_own, "core", swap)])

    query_rows, back_rows = make_latents(latents, w_query, cotangent, w_out)
    query_rings = ring_blocks(ring_gather(query_rows, "y"), "x")
    back_rings = ring_blocks(ring_gather(back_rows, "x"), "y")
    keys, values, normed = make_tokens(
        facts, mode_table, tokens, tokens_other, w_key, w_value, query_rows
    )

    place = jnp.stack([lax.axis_index(axis) for axis in ("x", "y", "core")]).astype(jnp.int32)
    weights, dprob, partial, own, both = attend(
        facts, place, query_rings, back_rings, keys, values
    )

    near = ring_gather(own[:3], "y")
    near_tops = near[:, 0]
    scale = jnp.exp(near_tops - jnp.max(near_tops, axis=0))
    near_sums = jnp.sum(near[:, 1:] * scale[:, None], axis=0)
    stats = ring_gather(jnp.concatenate([near_tops, near_sums]), "x")

    partials = lax.all_to_all(
        pass_on(partial, near_sums).reshape(chips, rows_here, width), XY, 0, 0, tiled=True
    )
    share = rows_here // heads
    lat_share = lax.dynamic_slice_in_dim(latents, lax.axis_index("mp") * share, share, 0)
    attn_rows = combine(place, partials, stats, lat_share)
    projected = jnp.dot(attn_rows, w_out, preferred_element_type=f32).astype(bf16)
    pieces = lax.all_to_all(projected.reshape(heads, share, lat_width), "mp", 0, 0, tiled=True)
    core = lax.axis_index("core")[None].astype(jnp.int32)
    keep, give = backward(core, stats, own, both, weights, dprob, normed, projected, chips)

    took = lax.ppermute(pass_on(give, pieces), "core", swap)
    mixed_share = add_pieces(pieces, lat_share, give)
    chip_grads = (keep.astype(f32) + took.astype(f32)).astype(bf16)
    head = lax.axis_index("mp")
    across = lax.ppermute(mixed_share, "mp", [(i, i ^ 4) for i in range(heads)])
    upper = head >= 4
    pair = jnp.stack(
        [jnp.where(upper, across, mixed_share), jnp.where(upper, mixed_share, across)]
    )
    quads = [pair] + [
        lax.ppermute(pair, "mp", [(i, i ^ move) for i in range(heads)]) for move in (1, 2, 3)
    ]
    mixed = place_pieces((head % 4)[None].astype(jnp.int32), quads).reshape(rows_here, lat_width)
    parts = lax.all_to_all(chip_grads, XY, 0, 0, tiled=True)
    out = jnp.sum(parts.astype(f32), axis=0)
    return mixed, out[:, :width], out[:, width:]


def solution(mesh):
    seq, heads = mesh.devices.shape
    side = 4
    fine = Mesh(mesh.devices.reshape(seq // (2 * side), side, 2, heads), SEQ + ("mp",))

    def body(*args):
        return on_device(*args, chips=seq // 2, heads=heads)

    in_specs = (
        P(SEQ, None),
        P(SEQ),
        P(SEQ),
        P(),
        P(SEQ, None),
        P(None, "mp"),
        P(None, "mp"),
        P(None, "mp"),
        P("mp", None),
        P(SEQ, None),
    )
    out_specs = (P(SEQ, None), P(SEQ, "mp"), P(SEQ, "mp"))
    return jax.shard_map(
        body, mesh=fine, in_specs=in_specs, out_specs=out_specs, check_vma=False
    )
```

```python
import functools

import jax
import jax.numpy as jnp
from jax import lax
from jax.experimental import pallas as pl
from jax.experimental.pallas import tpu as pltpu
from jax.sharding import Mesh, PartitionSpec as P

HD = 512
SCALE = HD ** (-0.5)
FLOOR = -1e30
XY = ("x", "y")
SEQ = ("x", "y", "core")
f32 = jnp.float32
bf16 = jnp.bfloat16


def normalize(values):
    mean = jnp.mean(values, axis=-1, keepdims=True)
    centred = values - mean
    spread = jnp.mean(centred * centred, axis=-1, keepdims=True)
    return centred * lax.rsqrt(spread + 1e-05)


def spread_out(block, axes, count):
    return lax.all_to_all(
        jnp.broadcast_to(block[None], (count,) + block.shape), axes, 0, 0, tiled=True
    )


def ring_blocks(block, axis):
    count = lax.axis_size(axis)
    return [block] + [
        lax.ppermute(block, axis, [(i, (i + k) % count) for i in range(count)])
        for k in range(1, count)
    ]


def ring_gather(block, axis):
    return jnp.stack(ring_blocks(block, axis))


def dot_nn(a, b):
    return jnp.dot(a, b, preferred_element_type=f32)


def dot_nt(a, b):
    return lax.dot_general(a, b, (((1,), (1,)), ((), ())), preferred_element_type=f32)


def dot_tn(a, b):
    return lax.dot_general(a, b, (((0,), (0,)), ((), ())), preferred_element_type=f32)


def far(*arrays):
    return [pltpu.with_memory_space_constraint(a, pltpu.HBM) for a in arrays]


def limits(bytes_wanted):
    return pltpu.CompilerParams(vmem_limit_bytes=bytes_wanted)


def latent_kernel(lat_ref, wq_ref, cot_ref, wo_ref, q_ref, b_ref, normed, total_q, total_b):
    step = pl.program_id(0)
    chunk = wq_ref.shape[0]

    @pl.when(step == 0)
    def _():
        normed[...] = normalize(lat_ref[...].astype(f32)).astype(bf16)
        total_q[...] = jnp.zeros_like(total_q)
        total_b[...] = jnp.zeros_like(total_b)

    columns = pl.ds(pl.multiple_of(step * chunk, chunk), chunk)
    total_q[...] += dot_nn(normed[:, columns], wq_ref[...])
    total_b[...] += dot_nt(cot_ref[...], wo_ref[...])

    @pl.when(step == pl.num_programs(0) - 1)
    def _():
        q_ref[...] = total_q[...].astype(bf16)
        b_ref[...] = total_b[...].astype(bf16)


def make_latents(latents, w_query, cotangent, w_out):
    rows, depth = latents.shape
    width = w_query.shape[1]
    steps = 2
    out = jax.ShapeDtypeStruct((rows, width), bf16)
    return pl.pallas_call(
        latent_kernel,
        grid=(steps,),
        in_specs=[
            pl.BlockSpec((rows, depth), lambda i: (0, 0)),
            pl.BlockSpec((depth // steps, width), lambda i: (i, 0)),
            pl.BlockSpec((rows, depth // steps), lambda i: (0, i)),
            pl.BlockSpec((width, depth // steps), lambda i: (0, i)),
        ],
        out_specs=[pl.BlockSpec((rows, width), lambda i: (0, 0))] * 2,
        out_shape=[out, out],
        scratch_shapes=[
            pltpu.VMEM((rows, depth), bf16),
            pltpu.VMEM((rows, width), f32),
            pltpu.VMEM((rows, width), f32),
        ],
        compiler_params=limits(32 << 20),
        cost_estimate=pl.CostEstimate(
            flops=4 * rows * depth * width,
            bytes_accessed=4 * (rows + width) * depth,
            transcendentals=rows,
        ),
    )(*far(latents, w_query, cotangent, w_out))


def token_kernel(
    facts_ref, table_ref, own_ref, other_ref, wk_ref, wv_ref, after_ref, k_ref, v_ref, n_ref
):
    def work(side, ref):
        for block in range(ref.shape[0] // 128):
            mode = facts_ref[side, block]
            place = pl.ds(block * 128, 128)
            raw = ref[place, :].astype(f32) + table_ref[pl.ds(mode, 1), :]
            n_ref[place, :] = normalize(raw).astype(bf16)

    @pl.when(pl.program_id(0) == 0)
    def _():
        work(0, own_ref)

    @pl.when(pl.program_id(0) == 1)
    def _():
        work(1, other_ref)

    k_ref[...] = dot_nn(n_ref[...], wk_ref[...]).astype(bf16)
    v_ref[...] = dot_nn(n_ref[...], wv_ref[...]).astype(bf16)


def make_tokens(facts, table, own, other, w_key, w_value, after):
    slots, in_width = own.shape
    width = w_key.shape[1]
    whole = lambda i: (0, 0)
    side = lambda i: (i, 0)
    return pl.pallas_call(
        token_kernel,
        grid=(2,),
        in_specs=[pl.BlockSpec(memory_space=pltpu.SMEM)]
        + [pl.BlockSpec(a.shape, whole) for a in (table, own, other, w_key, w_value)]
        + [pl.BlockSpec(memory_space=pl.ANY)],
        out_specs=[
            pl.BlockSpec((slots, width), side),
            pl.BlockSpec((slots, width), side),
            pl.BlockSpec((slots, in_width), side),
        ],
        out_shape=[
            pltpu.HBM((2 * slots, width), bf16),
            pltpu.HBM((2 * slots, width), bf16),
            pltpu.HBM((2 * slots, in_width), bf16),
        ],
        compiler_params=limits(40 << 20),
        cost_estimate=pl.CostEstimate(
            flops=8 * slots * in_width * width,
            bytes_accessed=4 * in_width * (2 * slots + width) + 8 * slots * width,
            transcendentals=2 * slots,
        ),
    )(facts, table, *far(own), other, *far(w_key, w_value), after)


def pass_kernel(array_ref, after_ref, out_ref):
    del array_ref, after_ref, out_ref


def pass_on(array, after):
    hbm = pl.BlockSpec(memory_space=pl.ANY)
    return pl.pallas_call(
        pass_kernel,
        in_specs=[hbm, hbm],
        out_specs=hbm,
        out_shape=jax.ShapeDtypeStruct(array.shape, array.dtype),
        input_output_aliases={0: 0},
    )(array, after)


def gathered(refs, here, rows):
    side_far, side_near = len(refs), refs[0].shape[0]
    for back_far, ref in enumerate(refs):
        for back_near in range(side_near):
            at_far = lax.rem(here[0] - back_far + side_far, side_far)
            at_near = lax.rem(here[1] - back_near + side_near, side_near)
            yield at_far, at_near, ref[back_near]


def scores_kernel(
    facts_ref, place_ref, q0_ref, q1_ref, q2_ref, q3_ref, b0_ref, b1_ref, b2_ref, b3_ref, k_ref,
    v_ref, w_ref, d_ref, part_ref, stat_ref, both_ref, ordered
):
    rows = w_ref.shape[0]
    slots, width = k_ref.shape
    share = q0_ref.shape[1]
    half = slots // 2
    last = facts_ref.shape[1] - 1
    step = pl.program_id(0)

    @pl.when(step == 0)
    def _():
        at_x, at_y = place_ref[0], place_ref[1]
        side = q0_ref.shape[0]
        for x, y, block in gathered((q0_ref, q1_ref, q2_ref, q3_ref), (at_x, at_y), share):
            first = pl.multiple_of((x * side + y) * share, share)
            ordered[pl.ds(first, share), :width] = block
        for y, x, block in gathered((b0_ref, b1_ref, b2_ref, b3_ref), (at_y, at_x), share):
            first = pl.multiple_of((x * side + y) * share, share)
            ordered[pl.ds(first, share), width:] = block

    taken = ordered[pl.ds(pl.multiple_of(step * rows, rows), rows), :]
    both_ref[...] = taken
    place = lax.broadcasted_iota(jnp.int32, (1, slots), 1)
    bound = jnp.where(place < half, facts_ref[0, last] * 128, half + facts_ref[1, last] * 128)
    scores = dot_nt(taken[:, :width], k_ref[...]) * SCALE
    scores = jnp.where(place < bound, scores, FLOOR)
    top = jnp.max(scores, axis=1, keepdims=True)
    weights = jnp.exp(scores - top)
    total = jnp.sum(weights, axis=1, keepdims=True)
    rounded = weights.astype(bf16)
    w_ref[...] = rounded
    dprob = dot_nt(taken[:, width:], v_ref[...])
    d_ref[...] = dprob
    cross = jnp.sum(weights * dprob, axis=1, keepdims=True)
    part_ref[...] = dot_nn(rounded, v_ref[...]).astype(bf16)
    lane = lax.broadcasted_iota(jnp.int32, (rows, 128), 1)
    stat_ref[...] = jnp.where(lane == 0, top, jnp.where(lane == 1, total, cross)).T[:8]


def attend(facts, place, query_rings, back_rings, keys, values):
    side, share, width = query_rings[0].shape
    lat = len(query_rings) * side * share
    slots = keys.shape[0]
    rows = 512
    whole = lambda i: (0, 0)
    chunk = lambda i: (i, 0)
    smem = pl.BlockSpec(memory_space=pltpu.SMEM)
    ring = pl.BlockSpec((side, share, width), lambda i: (0, 0, 0))
    return pl.pallas_call(
        scores_kernel,
        grid=(lat // rows,),
        in_specs=[smem, smem] + [ring] * 8 + [pl.BlockSpec((slots, width), whole)] * 2,
        out_specs=[
            pl.BlockSpec((rows, slots), chunk),
            pl.BlockSpec((rows, slots), chunk),
            pl.BlockSpec((rows, width), chunk),
            pl.BlockSpec((8, rows), lambda i: (0, i)),
            pl.BlockSpec((rows, 2 * width), chunk),
        ],
        out_shape=[
            pltpu.HBM((lat, slots), bf16),
            pltpu.HBM((lat, slots), f32),
            pltpu.HBM((lat, width), bf16),
            jax.ShapeDtypeStruct((8, lat), f32),
            pltpu.HBM((lat, 2 * width), bf16),
        ],
        scratch_shapes=[pltpu.VMEM((lat, 2 * width), bf16)],
        compiler_params=limits(48 << 20),
        cost_estimate=pl.CostEstimate(
            flops=6 * lat * slots * width,
            bytes_accessed=6 * lat * slots + 10 * lat * width + 4 * slots * width,
            transcendentals=lat * slots,
        ),
    )(facts, place, *query_rings, *back_rings, *far(keys, values))


def combine_rows(place_ref, part_ref, stat_ref, attn_ref):
    rows, width = attn_ref.shape
    side, lat = stat_ref.shape[0], stat_ref.shape[2]
    count = stat_ref.shape[1] - 2
    first = (place_ref[0] * count + place_ref[1]) * rows
    every = jnp.concatenate([stat_ref[back] for back in range(side)], axis=0)
    mine = pltpu.roll(every, lax.rem(lat - first, lat), 1)[:, :128]
    filler = jnp.zeros((128 - mine.shape[0], 128), f32)
    columns = jnp.concatenate([mine, filler], axis=0).T[:rows]
    stride = count + 2
    tops = [
        [columns[:, stride * x + y : stride * x + y + 1] for y in range(count)] for x in range(side)
    ]
    near = [functools.reduce(jnp.maximum, of_x) for of_x in tops]
    top = functools.reduce(jnp.maximum, near)
    total = jnp.zeros((rows, 1), f32)
    for x in range(side):
        at = stride * x + count
        total += jnp.exp(near[x] - top) * columns[:, at : at + 1]
    summed = jnp.zeros((rows, width), f32)
    for x in range(side):
        for y in range(count):
            at_x = lax.rem(place_ref[0] - x + side, side)
            at_y = lax.rem(place_ref[1] - y + count, count)
            part = part_ref[at_x * count + at_y].astype(f32)
            summed += part * jnp.exp(tops[x][y] - top)
    attn_ref[...] = (summed / total).astype(bf16)


def combine_kernel(place_ref, part_ref, stat_ref, w_ref, after_ref, out_ref, attn_ref):
    @pl.when(pl.program_id(0) == 0)
    def _():
        combine_rows(place_ref, part_ref, stat_ref, attn_ref)

    out_ref[...] = dot_nn(attn_ref[...], w_ref[...]).astype(bf16)


def combine(place, partials, stats, w_out, after):
    _, rows, width = partials.shape
    depth = w_out.shape[1]
    steps = 2
    return pl.pallas_call(
        combine_kernel,
        grid=(steps,),
        in_specs=[
            pl.BlockSpec(memory_space=pltpu.SMEM),
            pl.BlockSpec(partials.shape, lambda i: (0, 0, 0)),
            pl.BlockSpec(stats.shape, lambda i: (0, 0, 0)),
            pl.BlockSpec((width, depth // steps), lambda i: (0, i)),
            pl.BlockSpec(memory_space=pl.ANY),
        ],
        out_specs=pl.BlockSpec((rows, depth // steps), lambda i: (0, i)),
        out_shape=jax.ShapeDtypeStruct((rows, depth), bf16),
        scratch_shapes=[pltpu.VMEM((rows, width), bf16)],
        compiler_params=limits(24 << 20),
        cost_estimate=pl.CostEstimate(
            flops=2 * partials.size + 2 * rows * width * depth,
            bytes_accessed=2 * partials.size + 2 * depth * (rows + width),
            transcendentals=rows,
        ),
    )(place, partials, stats, *far(w_out), after)


def backward_kernel(
    core_ref, stat_ref, own_ref, both_ref, w_ref, d_ref, n_ref, after_ref, keep_ref,
    give_ref,    scaled, delta, grads, normed, result, arrived
):
    step = pl.program_id(0)
    width = both_ref.shape[1] // 2
    block = w_ref.shape[1]
    lat = both_ref.shape[0]
    fetch = pltpu.make_async_copy(n_ref, normed, arrived)

    @pl.when(step == 0)
    def _():
        fetch.start()
        every = stat_ref[...]
        count = every.shape[1] - 2
        tops = jnp.max(every[:, :count], axis=1)
        totals, crosses = every[:, count], every[:, count + 1]
        top = jnp.max(tops, axis=0, keepdims=True)
        factor = jnp.exp(tops - top)
        total = jnp.sum(factor * totals, axis=0, keepdims=True)
        mean = jnp.sum(factor * crosses, axis=0, keepdims=True) / total
        delta[...] = jnp.broadcast_to(mean, (128, lat)).T
        gain = jnp.exp(own_ref[0:1, :] - top) / total
        gain = jnp.broadcast_to(gain, (128, lat)).T
        gain = jnp.concatenate([gain] * (width // 128), axis=1)
        scaled[:, :width] = (both_ref[:, :width].astype(f32) * (gain * SCALE)).astype(bf16)
        scaled[:, width:] = (both_ref[:, width:].astype(f32) * gain).astype(bf16)

    mean = jnp.concatenate([delta[...]] * (block // 128), axis=1)
    dscore = (w_ref[...].astype(f32) * (d_ref[...] - mean)).astype(bf16)
    there = pl.ds(pl.multiple_of(step * block, block), block)
    grads[there, :width] = dot_tn(dscore, scaled[:, :width]).astype(bf16)
    grads[there, width:] = dot_tn(w_ref[...], scaled[:, width:]).astype(bf16)

    @pl.when(step == pl.num_programs(0) - 1)
    def _():
        fetch.wait()
        result[...] = dot_tn(normed[...], grads[...]).astype(bf16)
        chips, share = keep_ref.shape[0], keep_ref.shape[1]
        for core, refs in ((0, (keep_ref, give_ref)), (1, (give_ref, keep_ref))):

            @pl.when(core_ref[0] == core)
            def _():
                for chip in range(chips):
                    for part in range(2):
                        rows = pl.ds((2 * chip + part) * share, share)
                        refs[part][chip] = result[rows, :]


def backward(core, stats, own, both, weights, dprob, normed, after, chips):
    lat, slots = weights.shape
    width = both.shape[1] // 2
    in_width = normed.shape[1]
    share = in_width // (2 * chips)
    block = 256
    whole = lambda i: (0, 0)
    piece = pltpu.HBM((chips, share, 2 * width), bf16)
    piece_spec = pl.BlockSpec((chips, share, 2 * width), lambda i: (0, 0, 0))
    return pl.pallas_call(
        backward_kernel,
        grid=(slots // block,),
        in_specs=[
            pl.BlockSpec(memory_space=pltpu.SMEM),
            pl.BlockSpec(stats.shape, lambda i: (0, 0, 0)),
            pl.BlockSpec(own.shape, whole),
            pl.BlockSpec(both.shape, whole),
            pl.BlockSpec((lat, block), lambda i: (0, i)),
            pl.BlockSpec((lat, block), lambda i: (0, i)),
            pl.BlockSpec(memory_space=pl.ANY),
            pl.BlockSpec(memory_space=pl.ANY),
        ],
        out_specs=[piece_spec] * 2,
        out_shape=[piece] * 2,
        scratch_shapes=[
            pltpu.VMEM((lat, 2 * width), bf16),
            pltpu.VMEM((lat, 128), f32),
            pltpu.VMEM((slots, 2 * width), bf16),
            pltpu.VMEM(normed.shape, bf16),
            pltpu.VMEM((in_width, 2 * width), bf16),
            pltpu.SemaphoreType.DMA,
        ],
        compiler_params=limits(40 << 20),
        cost_estimate=pl.CostEstimate(
            flops=4 * slots * width * (lat + in_width),
            bytes_accessed=6 * lat * slots + 2 * in_width * (slots + 2 * width) + 4 * width * lat,
            transcendentals=lat,
        ),
    )(core, stats, own, *far(both, weights, dprob, normed), after)


def add_kernel(pieces_ref, lat_ref, after_ref, out_ref):
    total = lat_ref[...].astype(f32) + jnp.sum(pieces_ref[...].astype(f32), axis=0)
    out_ref[...] = total.astype(bf16)


def add_pieces(pieces, latents, after):
    vmem = pl.BlockSpec(memory_space=pltpu.VMEM)
    return pl.pallas_call(
        add_kernel,
        in_specs=[vmem, vmem, pl.BlockSpec(memory_space=pl.ANY)],
        out_specs=vmem,
        out_shape=jax.ShapeDtypeStruct(latents.shape, bf16),
        cost_estimate=pl.CostEstimate(
            flops=pieces.size, bytes_accessed=2 * pieces.size, transcendentals=0
        ),
    )(pieces, latents, after)


def place_kernel(low_ref, v0_ref, v1_ref, v2_ref, v3_ref, out_ref):
    refs = (v0_ref, v1_ref, v2_ref, v3_ref)
    low = low_ref[0]
    for move, ref in enumerate(refs):
        at = jnp.where(move & 1, 1 - low % 2, low % 2) + 2 * jnp.where(
            move & 2, 1 - low // 2, low // 2
        )
        for high in range(ref.shape[0]):
            out_ref[high * len(refs) + at] = ref[high]


def place_pieces(low, pieces):
    pair, rows, width = pieces[0].shape
    vmem = pl.BlockSpec(memory_space=pltpu.VMEM)
    shape = (pair * len(pieces), rows, width)
    return pl.pallas_call(
        place_kernel,
        in_specs=[pl.BlockSpec(memory_space=pltpu.SMEM)] + [vmem] * len(pieces),
        out_specs=vmem,
        out_shape=jax.ShapeDtypeStruct(shape, bf16),
        compiler_params=limits(16 << 20),
        cost_estimate=pl.CostEstimate(
            flops=0, bytes_accessed=4 * pair * len(pieces) * rows * width, transcendentals=0
        ),
    )(low, *pieces)


def on_device(
    tokens,
    block_modality,
    live_blocks,
    mode_table,
    latents,
    w_query,
    w_key,
    w_value,
    w_out,
    cotangent,
    *,
    chips,
    heads,
):
    tok_count, in_width = tokens.shape
    width = w_key.shape[1]
    rows_here, lat_width = latents.shape
    lat_half = chips * rows_here
    swap = [(0, 1), (1, 0)]

    tokens_other = lax.ppermute(tokens, "core", swap)
    facts_own = jnp.concatenate([block_modality, live_blocks])
    facts = jnp.stack([facts_own, lax.ppermute(facts_own, "core", swap)])

    query_rows, back_rows = make_latents(latents, w_query, cotangent, w_out)
    query_rings = ring_blocks(ring_gather(query_rows, "y"), "x")
    back_rings = ring_blocks(ring_gather(back_rows, "x"), "y")
    keys, values, normed = make_tokens(
        facts, mode_table, tokens, tokens_other, w_key, w_value, query_rows
    )

    place = jnp.stack([lax.axis_index(axis) for axis in ("x", "y", "core")]).astype(jnp.int32)
    weights, dprob, partial, own, both = attend(
        facts, place, query_rings, back_rings, keys, values
    )

    near = ring_gather(own[:3], "y")
    near_tops = near[:, 0]
    scale = jnp.exp(near_tops - jnp.max(near_tops, axis=0))
    near_sums = jnp.sum(near[:, 1:] * scale[:, None], axis=0)
    stats = ring_gather(jnp.concatenate([near_tops, near_sums]), "x")

    partials = lax.all_to_all(
        pass_on(partial, near_sums).reshape(chips, rows_here, width), XY, 0, 0, tiled=True
    )
    share = rows_here // heads
    lat_share = lax.dynamic_slice_in_dim(latents, lax.axis_index("mp") * share, share, 0)
    projected = combine(place, partials, stats, w_out, lat_share)
    pieces = lax.all_to_all(projected.reshape(heads, share, lat_width), "mp", 0, 0, tiled=True)
    core = lax.axis_index("core")[None].astype(jnp.int32)
    keep, give = backward(core, stats, own, both, weights, dprob, normed, projected, chips)

    took = lax.ppermute(pass_on(give, pieces), "core", swap)
    mixed_share = add_pieces(pieces, lat_share, give)
    chip_grads = (keep.astype(f32) + took.astype(f32)).astype(bf16)
    head = lax.axis_index("mp")
    across = lax.ppermute(mixed_share, "mp", [(i, i ^ 4) for i in range(heads)])
    upper = head >= 4
    pair = jnp.stack(
        [jnp.where(upper, across, mixed_share), jnp.where(upper, mixed_share, across)]
    )
    quads = [pair] + [
        lax.ppermute(pair, "mp", [(i, i ^ move) for i in range(heads)]) for move in (1, 2, 3)
    ]
    mixed = place_pieces((head % 4)[None].astype(jnp.int32), quads).reshape(rows_here, lat_width)
    parts = lax.all_to_all(chip_grads, XY, 0, 0, tiled=True)
    out = jnp.sum(parts.astype(f32), axis=0)
    return mixed, out[:, :width], out[:, width:]


def solution(mesh):
    seq, heads = mesh.devices.shape
    side = 4
    fine = Mesh(mesh.devices.reshape(seq // (2 * side), side, 2, heads), SEQ + ("mp",))

    def body(*args):
        return on_device(*args, chips=seq // 2, heads=heads)

    in_specs = (
        P(SEQ, None),
        P(SEQ),
        P(SEQ),
        P(),
        P(SEQ, None),
        P(None, "mp"),
        P(None, "mp"),
        P(None, "mp"),
        P("mp", None),
        P(SEQ, None),
    )
    out_specs = (P(SEQ, None), P(SEQ, "mp"), P(SEQ, "mp"))
    return jax.shard_map(
        body, mesh=fine, in_specs=in_specs, out_specs=out_specs, check_vma=False
    )
```
